256 devices in a mesh: band: 4 (over x_hi, core), grid: 64 (over x_lo, z, y).
Axes of the slice: x: 4 (x_hi: 2, x_lo: 2; x = x_hi * 2 + x_lo), y: 4, z: 8, core: 2. Of those that a mesh axis runs over, the one named last changes fastest.
Arguments:
- orbitals: float32 [768, 16, 16, 512], P('grid', None, None, 'band'), may hold values from -24 to 24
- potential: float32 [768, 16, 16], P('grid'), may hold values from -3 to -1
- projectors: float32 [256, 8, 13, 256], P('grid'), may hold values from -0.109375 to 0.109375
- atom_planes: int32 [256, 13], P('grid'), may hold values from 0 to 23, as said below
- kb_energy: float32 [8], replicated, may hold values from 1 to 4
Outputs:
- filtered: float32 [768, 16, 16, 512], P('grid', None, None, 'band')
- correlation_gram: float32 [512, 512], P('band')
The draws below stay inside these ranges and needn't reach their ends.
Inputs may be any that keep to these rules, and one draw needn't show every extreme that they name: `atom_planes`: each atom's row holds 13 consecutive plane numbers; the first atom starts at plane 0 and the last atom at plane 12 - 1.
All inputs are finite; a program needn't handle non-finite values.
Results may differ from the reference program's by a relative error of at most 0.0003.
Values sent between devices are 32-bit elements; how exact they have to be, the bound alone decides.
A program may use at most 128 MiB of HBM per device.

```python
import jax
import jax.numpy as jnp
from jax import lax

NORB = 512
CX = 12
NY = 16
NZ = 16
ATOM_DEV = 4
NPJ = 8
NBLK = 13
DEGREE = 4
NX = 768
NATOM = 256
CELLS = 196608


def draw_atom_planes(key, part):
    offsets = jax.random.randint(key, (NATOM,), 0, CX, dtype=jnp.int32)
    offsets = offsets.at[0].set(0).at[NATOM - 1].set(CX - 1)
    return offsets[:, None] + jnp.arange(NBLK, dtype=jnp.int32)[None, :]


def block_scale(own_key, extent, shards, least, top_value):
    factor_of, own = 1.0, jax.random.fold_in(own_key, 6)
    for dim, parts in shards:
        draws = jnp.exp(jax.random.uniform(jax.random.fold_in(own, dim), (parts,), jnp.float32, least / len(shards), top_value / len(shards)))
        factor_of = factor_of * jnp.repeat(draws, extent[dim] // parts).reshape([-1 if axis == dim else 1 for axis in range(len(extent))])
    return factor_of


def noise(rng, dims, spread, limit, cuts=(), kind=jnp.bfloat16):
    array = spread * jax.random.normal(rng, dims, jnp.float32)
    if cuts:
        array = array * block_scale(rng, dims, cuts, -0.22, 0.18)
    return jnp.clip(array, -limit, limit).astype(kind)


def setup_inputs(seed: int = 0) -> dict:
    streams_of = jax.random.split(jax.random.key(seed), 6)
    orbitals = noise(streams_of[0], (NX, NY, NZ, NORB), 4.0, 24.0, ((0, 64), (3, 4)), jnp.float32)
    potential = jnp.clip(-3.0 + 2.0 * jax.random.uniform(streams_of[1], (NX, NY, NZ), jnp.float32) ** block_scale(streams_of[1], (NX, NY, NZ), ((0, 64),), -0.2, 0.2), -3.0, -1.0)
    projectors = noise(streams_of[2], (NATOM, NPJ, NBLK, NY * NZ), (NBLK * NY * NZ) ** -0.5, 0.109375, ((0, 64),), jnp.float32)
    atom_planes = draw_atom_planes(jax.random.fold_in(streams_of[5], 71), 0)
    kb_energy = jnp.clip(jax.random.uniform(streams_of[4], (NPJ,), jnp.float32, 1.0, 4.0), 1.0, 4.0)
    return dict(orbitals=orbitals, potential=potential, projectors=projectors, atom_planes=atom_planes, kb_energy=kb_energy)


WEIGHTS = (-5369.0 / 1800.0, 12.0 / 7.0, -15.0 / 56.0, 10.0 / 189.0, -1.0 / 112.0, 2.0 / 1925.0, -1.0 / 16632.0)
LOWER = -4.0
CUTOFF = 1.0
UPPER = 16.0
PRECISE = lax.Precision.HIGHEST


def filter_terms(degree):
    half_span = (UPPER - CUTOFF) / 2.0
    middle = (UPPER + CUTOFF) / 2.0
    sigma_now = half_span / (LOWER - middle)
    sigma_first = sigma_now
    scales = [sigma_now / half_span]
    recall = [0.0]
    for level in range(1, degree):
        sigma_next = 1.0 / (2.0 / sigma_first - sigma_now)
        scales.append(2.0 * sigma_next / half_span)
        recall.append(sigma_now * sigma_next)
        sigma_now = sigma_next
    return middle, scales, recall


def second_roll(values, along):
    summed = WEIGHTS[0] * values
    for reach in range(1, 7):
        summed = summed + WEIGHTS[reach] * (jnp.roll(values, reach, along) + jnp.roll(values, -reach, along))
    return summed


def nonlocal_term(values, projectors, atom_planes, kb_energy):
    offsets = (jnp.arange(NATOM, dtype=jnp.int32) // ATOM_DEV) * CX - 6

    def add_atom(accum, atom_data):
        chi_rows, rows_here, offset = atom_data
        plane_ids = ((offset + rows_here) % NX).astype(jnp.int32)
        gathered = values[plane_ids].reshape(-1, NORB)
        chi_flat = chi_rows.reshape(NPJ, -1)
        correlation = jnp.dot(chi_flat, gathered, precision=PRECISE) * kb_energy[:, None]
        contrib = lax.dot_general(chi_flat, correlation, (((0,), (0,)), ((), ())), precision=PRECISE)
        return accum.at[plane_ids].add(contrib.reshape(NBLK, NY, NZ, NORB)), None

    accum, unused = lax.scan(add_atom, jnp.zeros_like(values), (projectors, atom_planes, offsets))
    return accum


def hamiltonian(values, potential, projectors, atom_planes, kb_energy):
    lap = second_roll(values, 0) + second_roll(values, 1) + second_roll(values, 2)
    local_part = -0.5 * lap + potential[..., None] * values
    return local_part + nonlocal_term(values, projectors, atom_planes, kb_energy)


def reference(orbitals, potential, projectors, atom_planes, kb_energy):
    middle, scales, recall = filter_terms(DEGREE)
    previous = orbitals
    current = orbitals
    for level in range(DEGREE):
        applied = hamiltonian(current, potential, projectors, atom_planes, kb_energy)
        result = scales[level] * (applied - middle * current)
        if level > 0:
            result = result - recall[level] * previous
        previous = current
        current = result
    flattened = current.reshape(-1, NORB)
    correlation_gram = lax.dot_general(flattened, flattened, (((0,), (0,)), ((), ())), precision=PRECISE) * (1.0 / CELLS)
    return current, correlation_gram
```

```python
import functools

import jax
import jax.numpy as jnp
import ml_dtypes
import numpy as np
from jax import lax
from jax.experimental import pallas as pl
from jax.experimental.pallas import tpu as pltpu
from jax.sharding import PartitionSpec as P

DEGREE = 4
CX = 12
ROWS = 256
ORB = 128
QR = 64
NPROJ = 32
CELLS = 196608
CH_IN = 3
CH_OUT = 4
WEIGHTS = (
    -5369.0 / 1800.0,
    12.0 / 7.0,
    -15.0 / 56.0,
    10.0 / 189.0,
    -1.0 / 112.0,
    2.0 / 1925.0,
    -1.0 / 16632.0,
)
HALFW = tuple(-0.5 * w for w in WEIGHTS)
LOWER = -4.0
CUTOFF = 1.0
UPPER = 16.0
F32 = jnp.float32
BF16 = jnp.bfloat16
MESH = pl.DeviceIdType.MESH


def filter_terms(degree):
    half_span = (UPPER - CUTOFF) / 2.0
    middle = (UPPER + CUTOFF) / 2.0
    sigma_now = half_span / (LOWER - middle)
    sigma_first = sigma_now
    scales = [sigma_now / half_span]
    recall = [0.0]
    for level in range(1, degree):
        sigma_next = 1.0 / (2.0 / sigma_first - sigma_now)
        scales.append(2.0 * sigma_next / half_span)
        recall.append(sigma_now * sigma_next)
        sigma_now = sigma_next
    return middle, scales, recall


def plane_laplacian():
    mat = np.zeros((16, 16, 16, 16), np.float64)
    for a in range(16):
        for b in range(16):
            for r in range(1, 7):
                for sign in (-1, 1):
                    mat[a, b, (a + sign * r) % 16, b] += HALFW[r]
                    mat[a, b, a, (b + sign * r) % 16] += HALFW[r]
    mat = mat.reshape(256, 256).astype(np.float32)
    high = mat.astype(ml_dtypes.bfloat16)
    low = (mat - high.astype(np.float32)).astype(ml_dtypes.bfloat16)
    return np.stack([high, low])


def split(value):
    high = value.astype(BF16)
    return high, (value - high.astype(F32)).astype(BF16)


def dot(a, b):
    return jnp.dot(a, b, preferred_element_type=F32)


def dot3(a_high, a_low, b_high, b_low):
    return dot(a_high, b_high) + (dot(a_high, b_low) + dot(a_low, b_high))


def dot_t(a, b):
    return lax.dot_general(a, b, (((0,), (0,)), ((), ())), preferred_element_type=F32)


def lane_block(rows):
    return lax.broadcasted_iota(jnp.int32, (rows, ORB), 1) // 32


def roll(value, blocks):
    blocks = blocks % 4
    return value if blocks == 0 else pltpu.roll(value, 32 * blocks, 1)


def transpose_blocks(parts):
    blk = lane_block(parts[0].shape[0])
    low = blk < 2
    even = (blk % 2) == 0
    a0, a1, a2, a3 = parts
    b0 = jnp.where(low, a0, roll(a2, 2))
    b2 = jnp.where(low, roll(a0, 2), a2)
    b1 = jnp.where(low, a1, roll(a3, 2))
    b3 = jnp.where(low, roll(a1, 2), a3)
    return (
        jnp.where(even, b0, roll(b1, 1)),
        jnp.where(even, roll(b0, 3), b1),
        jnp.where(even, b2, roll(b3, 1)),
        jnp.where(even, roll(b2, 3), b3),
    )


def loop(start, stop, body):
    lax.fori_loop(start, stop, lambda i, c: (body(i), c)[1], 0)


def kernel(
    orb, pot, payload, kbt, lap, out, gram,
    x_in, r_in, pg, potg, cm, rim, chi_h, chi_l, cht_h, cht_l, pc_mat, wide, base_lv,
    halo_s, halo_r, part, pc_s, pc_r, cc_h, cc_l, fix,
    x_out, r_out, filt, filt_c, xr, xr2, gb, yr, sb, sr, st, xt, tb, go,
    in_s, in_r, chi_s, chi_r, cor_s, cor_r, pot_s, pot_r, rim_s, rim_r, hal_s, hal_r, par_s, par_r,
    out_s, out_r, fc_s, fc_r, xs_s, xs_r, rl_s, rl_r, ys_s, ys_r, ss_s, ss_r, xh_s, xh_r, sg_s, sg_r, yg_s, yg_r, loc, hbm,
):
    middle, scales, recall = filter_terms(DEGREE)
    b = lax.axis_index("band")
    g = lax.axis_index("grid")
    s, y = g // 4, g % 4
    xh, c = b // 2, b % 2
    core = (2 * xh + 1 - c, g)
    across = (2 * (1 - xh) + c, g)
    cross = (2 * (1 - xh) + 1 - c, g)
    up = (b, (g + 4) % 64)
    down = (b, (g + 60) % 64)
    ypeer = [None] + [(b, 4 * s + (y + k) % 4) for k in range(1, 4)]
    speer = [None] + [(b, (g + 4 * d) % 64) for d in range(1, 16)]
    pending = []

    def rcopy(src, dst, ssem, rsem, dev):
        cp = pltpu.make_async_remote_copy(
            src_ref=src, dst_ref=dst, send_sem=ssem, recv_sem=rsem, device_id=dev, device_id_type=MESH
        )
        cp.start()
        pending.append(cp)
        return cp

    barrier = pltpu.get_barrier_semaphore()
    friends = ypeer[1:] + speer[1:] + [core, across, cross]
    for dev in friends:
        pl.semaphore_signal(barrier, inc=1, device_id=dev, device_id_type=MESH)
    pl.semaphore_wait(barrier, len(friends))

    half = pl.ds(27 * c, 27)
    chi_in = [None]
    pot_in = [None]
    for k in range(1, 4):
        chi_in.append(rcopy(payload.at[half], pg.at[y, half], chi_s.at[k - 1], chi_r.at[k - 1], ypeer[k]))
        pot_in.append(rcopy(pot, potg.at[y], pot_s.at[k - 1], pot_r.at[k - 1], ypeer[k]))
    own_pg = pltpu.make_async_copy(payload, pg.at[y], loc.at[0])
    own_pg.start()
    own_pot = pltpu.make_async_copy(pot, potg.at[y], loc.at[1])
    own_pot.start()

    span = CX // CH_IN
    orb_in = []
    orb_own = []

    def pack_in(i):
        parts = [orb[i, pl.ds(QR * q, QR), :] for q in range(4)]
        for k, value in enumerate(transpose_blocks(parts)):
            x_in[k, i] = value

    for ch in range(CH_IN):
        loop(span * ch, span * (ch + 1), pack_in)
        planes = pl.ds(span * ch, span)
        row = []
        for k in range(1, 4):
            row.append(
                rcopy(
                    x_in.at[(y + k) % 4, planes], r_in.at[y, planes],
                    in_s.at[k - 1, ch], in_r.at[k - 1, ch], ypeer[k],
                )
            )
        orb_in.append(row)
        own = pltpu.make_async_copy(x_in.at[y, planes], r_in.at[y, planes], loc.at[2 + ch])
        own.start()
        orb_own.append(own)

    for slot in range(4, 8):
        potg[slot] = jnp.zeros((16, ROWS), F32)
    own_pot.wait()
    for k in range(1, 4):
        pot_in[k].wait_recv()
    pot_t = potg[...].reshape(128, ROWS).T
    p_high = pot_t.astype(BF16)
    rest = pot_t - p_high.astype(F32)
    p_mid = rest.astype(BF16)
    p_low = (rest - p_mid.astype(F32)).astype(BF16)
    centre = 3.0 * HALFW[0] - middle
    e_row = lax.broadcasted_iota(jnp.int32, (128, ORB), 0)
    e_same = (e_row // 16) == lane_block(128)

    def spread_pot(i):
        pick = jnp.where(e_same & (e_row % 16 == i), 1.0, 0.0).astype(BF16)
        pc_mat[i] = (dot(p_high, pick) + (dot(p_mid, pick) + dot(p_low, pick))) + centre

    loop(0, CX, spread_pot)

    cor_in = [None]
    own_pg.wait()
    for k in range(1, 4):
        chi_in[k].wait_recv()
        src = (y + 4 - k) % 4
        cor_in.append(rcopy(pg.at[src, half], pg.at[src, half], cor_s.at[k - 1], cor_r.at[k - 1], core))
    for k in range(1, 4):
        cor_in[k].wait_recv()

    def place(dom):
        for j in range(4):
            start = pg[dom, 52 + j // 2, :, pl.ds(128 * (j % 2), 128)]
            bits = {}
            left = start
            for size in (8, 4, 2, 1):
                bits[size] = left >= (size - 0.5)
                left = jnp.where(bits[size], left - size, left)
            for lh in range(2):
                lanes = pl.ds(128 * lh, 128)
                zero = jnp.zeros((8, 128), F32)
                rows = [pg[dom, 13 * j + n, :, lanes] for n in range(13)]
                for size in (1, 2, 4, 8):
                    count = min(len(rows) + size, 24)
                    at = lambda n, rows=rows: rows[n] if 0 <= n < len(rows) else zero
                    rows = [jnp.where(bits[size], at(n - size), at(n)) for n in range(count)]
                for n in range(24):
                    cm[dom, n, pl.ds(8 * j, 8), lanes] = rows[n]

    loop(0, 4, place)
    rim_in = [
        rcopy(cm.at[3, pl.ds(18, 6)], rim.at[0], rim_s.at[0], rim_r.at[0], up),
        rcopy(cm.at[0, pl.ds(0, 6)], rim.at[1], rim_s.at[1], rim_r.at[1], down),
    ]
    for cp in rim_in:
        cp.wait_recv()

    def make_chi(i, beside):
        mat = jnp.concatenate([cm[d, i + 6] for d in range(4)] + beside, axis=0)
        chi_h[i], chi_l[i] = split(mat)
        cht_h[i], cht_l[i] = split(mat.T)

    loop(0, 6, lambda i: make_chi(i, [rim[0, i]] + [cm[d, i + 18] for d in range(3)]))
    loop(6, 12, lambda i: make_chi(i, [cm[d, i - 6] for d in range(1, 4)] + [rim[1, i - 6]]))

    def unpack_in(i):
        parts = [r_in[m, i] for m in range(4)]
        for q, value in enumerate(transpose_blocks(parts)):
            wide[0, 6 + i, pl.ds(QR * q, QR), :] = value
            wide[1, 6 + i, pl.ds(QR * q, QR), :] = value

    for ch in range(CH_IN):
        orb_own[ch].wait()
        for cp in orb_in[ch]:
            cp.wait_recv()
        loop(span * ch, span * (ch + 1), unpack_in)

    blk64 = lane_block(QR)
    blk32 = lane_block(NPROJ)
    for lv in range(DEGREE):
        cur, nxt = lv % 2, 1 - lv % 2
        scale, back = scales[lv], recall[lv]

        def pack_halo(i):
            high = jnp.zeros((QR, ORB), F32)
            low = jnp.zeros((QR, ORB), F32)
            for q in range(4):
                high = jnp.where(blk64 == q, roll(wide[cur, 12 + i, pl.ds(QR * q, QR), :], q - 3), high)
                low = jnp.where(blk64 == q, roll(wide[cur, 6 + i, pl.ds(QR * q, QR), :], q), low)
            halo_s[lv, 0, i] = high
            halo_s[lv, 1, i] = low

        loop(0, 6, pack_halo)
        halo_in = [
            rcopy(halo_s.at[lv, 0], halo_r.at[lv, 0], hal_s.at[lv, 0], hal_r.at[lv, 0], up),
            rcopy(halo_s.at[lv, 1], halo_r.at[lv, 1], hal_s.at[lv, 1], hal_r.at[lv, 1], down),
        ]

        def rims(i):
            for q in range(4):
                rows = pl.ds(QR * q, QR)
                wide[cur, i, rows, :] = jnp.where(blk64 == 0, 0.0, roll(wide[cur, 12 + i, rows, :], 1))
                wide[cur, 18 + i, rows, :] = jnp.where(blk64 == 3, 0.0, roll(wide[cur, 6 + i, rows, :], 3))

        loop(0, 6, rims)
        part[...] = jnp.zeros_like(part)

        def local(i):
            high, low = split(wide[cur, 6 + i])
            partial = dot3(chi_h[i], chi_l[i], high, low)
            part[0] += partial[:128]
            part[1 + i // 6] += partial[128:]
            base_lv[...] = dot3(lap[0], lap[1], high, low)
            for q in range(4):
                rows = pl.ds(QR * q, QR)
                value = base_lv[rows, :] + pc_mat[i, rows, :] * wide[cur, 6 + i, rows, :]
                for r in range(1, 7):
                    value = value + HALFW[r] * (wide[cur, 6 + i + r, rows, :] + wide[cur, 6 + i - r, rows, :])
                value = scale * value
                if lv > 0:
                    value = value - back * wide[nxt, 6 + i, rows, :]
                wide[nxt, 6 + i, rows, :] = value

        loop(0, CX, local)
        for n in range(3):
            packed = jnp.zeros((NPROJ, ORB), F32)
            for d in range(4):
                packed = jnp.where(blk32 == d, part[n, pl.ds(NPROJ * d, NPROJ), :], packed)
            pc_s[lv, n] = packed
        part_in = [
            rcopy(pc_s.at[lv], pc_r.at[lv, 0], par_s.at[lv, 0], par_r.at[lv, 0], up),
            rcopy(pc_s.at[lv], pc_r.at[lv, 1], par_s.at[lv, 1], par_r.at[lv, 1], down),
        ]
        for cp in halo_in:
            cp.wait_recv()

        for i in range(6):
            low = HALFW[i + 1] * halo_r[lv, 0, 5]
            for r in range(i + 2, 7):
                low = low + HALFW[r] * halo_r[lv, 0, 6 + i - r]
            fix[i] = low
            high = HALFW[6 - i] * halo_r[lv, 1, 0]
            for r in range(7 - i, 7):
                high = high + HALFW[r] * halo_r[lv, 1, i + r - 6]
            fix[6 + i] = high
        for cp in part_in:
            cp.wait_recv()
        own, dn, hi = pc_s[lv, 0], pc_s[lv, 1], pc_s[lv, 2]
        corr = (
            own
            + jnp.where(blk32 == 0, roll(pc_r[lv, 0, 2], 1), roll(hi, 1))
            + jnp.where(blk32 == 3, roll(pc_r[lv, 1, 1], 3), roll(dn, 3))
        )
        corr_low = roll(pc_r[lv, 0, 0], 1) + roll(pc_r[lv, 0, 2], 2) + dn
        corr_high = roll(pc_r[lv, 1, 0], 3) + roll(pc_r[lv, 1, 1], 2) + hi
        beside_low = jnp.where(blk32 == 0, corr_low, roll(corr, 1))
        beside_high = jnp.where(blk32 == 3, corr_high, roll(corr, 3))
        energy = jnp.concatenate([kbt[...]] * 4, axis=0) * scale
        for n, value in enumerate((corr, beside_low, beside_high)):
            high, low = split(value * energy)
            high, low = high.astype(F32), low.astype(F32)
            for d in range(4):
                rows = pl.ds(NPROJ * d, NPROJ)
                cc_h[n, rows, :] = jnp.where(blk32 == d, high, 0.0).astype(BF16)
                cc_l[n, rows, :] = jnp.where(blk32 == d, low, 0.0).astype(BF16)

        def finish(i, n, edge):
            ch = jnp.concatenate([cc_h[0], cc_h[n]], axis=0)
            cl = jnp.concatenate([cc_l[0], cc_l[n]], axis=0)
            base_lv[...] = dot3(cht_h[i], cht_l[i], ch, cl)
            for q in range(4):
                rows = pl.ds(QR * q, QR)
                more = jnp.where(blk64 == edge, roll(fix[i], edge - q), 0.0)
                wide[nxt, 6 + i, rows, :] = wide[nxt, 6 + i, rows, :] + (base_lv[rows, :] + scale * more)

        loop(0, 6, lambda i: finish(i, 1, 0))
        loop(6, 12, lambda i: finish(i, 2, 3))

    last = DEGREE % 2

    def pack_out(i):
        parts = [wide[last, 6 + i, pl.ds(QR * q, QR), :] for q in range(4)]
        for k, value in enumerate(transpose_blocks(parts)):
            x_out[k, i] = value

    def first_plane(ch):
        return (6 * (1 - xh) if ch < 2 else 6 * xh) + 3 * (ch % 2)

    back_in = []
    back_own = []
    for ch in range(CH_OUT):
        first = first_plane(ch)
        loop(0, 3, lambda i: pack_out(first + i))
        planes = pl.ds(first, 3)
        row = []
        for k in range(1, 4):
            row.append(
                rcopy(
                    x_out.at[(y + k) % 4, planes], r_out.at[y, planes],
                    out_s.at[k - 1, ch], out_r.at[k - 1, ch], ypeer[k],
                )
            )
        back_in.append(row)
        own = pltpu.make_async_copy(x_out.at[y, planes], r_out.at[y, planes], loc.at[8 + ch])
        own.start()
        back_own.append(own)

    def unpack_out(i):
        parts = [r_out[m, i] for m in range(4)]
        for q, value in enumerate(transpose_blocks(parts)):
            filt[i, pl.ds(QR * q, QR), :] = value

    fc_in = []
    x_recv = []
    stores = []
    for ch in range(CH_OUT):
        first = first_plane(ch)
        back_own[ch].wait()
        for cp in back_in[ch]:
            cp.wait_recv()
        loop(0, 3, lambda i: unpack_out(first + i))
        planes = pl.ds(first, 3)
        if ch < 2:
            x_recv.append(rcopy(filt.at[planes], xr.at[pl.ds(3 * ch, 3)], xs_s.at[ch], xs_r.at[ch], across))
        fc_in.append(rcopy(filt.at[planes], filt_c.at[planes], fc_s.at[ch], fc_r.at[ch], core))
        store = pltpu.make_async_copy(filt.at[planes], out.at[planes], hbm.at[ch])
        store.start()
        stores.append(store)

    gb[...] = jnp.zeros_like(gb)

    def gram_step(slot, lhs, rhs):
        a_high, a_low = split(lhs)
        parts = [split(value) for value in rhs]
        r_high = jnp.concatenate([p[0] for p in parts], axis=1)
        r_low = jnp.concatenate([p[1] for p in parts], axis=1)
        value = dot_t(a_high, r_high) + (dot_t(a_high, r_low) + dot_t(a_low, r_high))
        gb[slot] += value[:, :128]
        gb[slot + 1] += value[:, 128:]

    for cp in fc_in:
        cp.wait_recv()
    loop(0, CX, lambda i: gram_step(0, filt[i], [filt[i], filt_c[i]]))
    relay = []
    for ch in range(2):
        x_recv[ch].wait_recv()
        planes = pl.ds(3 * ch, 3)
        relay.append(rcopy(xr.at[planes], xr2.at[planes], rl_s.at[ch], rl_r.at[ch], core))
    for ch in range(2):
        relay[ch].wait_recv()
        loop(3 * ch, 3 * ch + 3, lambda i: gram_step(2, filt[6 * xh + i], [xr[i], xr2[i]]))
    for n in (2, 3):
        gb[n] = jnp.where(xh == 1, gb[n].T, gb[n])

    y_in = []
    for k in range(1, 4):
        y_in.append(rcopy(gb.at[(y + k) % 4], yr.at[k - 1], ys_s.at[k - 1], ys_r.at[k - 1], ypeer[k]))
    for cp in y_in:
        cp.wait_recv()
    sb[...] = (gb[y] + (yr[0] + (yr[1] + yr[2]))).reshape(16, 8, 128)
    for d in range(1, 16):
        cp = pltpu.make_async_remote_copy(
            src_ref=sb.at[(s + d) % 16], dst_ref=sr.at[d - 1], send_sem=ss_s, recv_sem=ss_r,
            device_id=speer[d], device_id_type=MESH,
        )
        cp.start()
    pltpu.make_async_copy(sr, sr, ss_r).wait()
    tile = sb[s]
    for d in range(15):
        tile = tile + sr[d]
    st[...] = tile
    partner = (2 * (1 - xh) + (c + y // 3 * (1 - 2 * c)), g)
    xh_in = rcopy(st, xt, xh_s.at[0], xh_r.at[0], partner)
    xh_in.wait_recv()
    tb[s] = tile + jnp.where(y >= 2, xt[...], 0.0)
    for d in range(1, 16):
        cp = pltpu.make_async_remote_copy(
            src_ref=tb.at[s], dst_ref=tb.at[s], send_sem=sg_s, recv_sem=sg_r,
            device_id=speer[d], device_id_type=MESH,
        )
        cp.start()
    pltpu.make_async_copy(sr, sr, sg_r).wait()
    go[y] = tb[...].reshape(128, 128) * (1.0 / CELLS)
    yg_in = []
    for k in range(1, 4):
        yg_in.append(rcopy(go.at[y], go.at[y], yg_s.at[k - 1], yg_r.at[k - 1], ypeer[k]))
    for cp in yg_in:
        cp.wait_recv()
    gram[b] = go[0]
    gram[core[0]] = go[1]
    gram[across[0]] = jnp.where(xh == 1, go[2].T, go[2])
    gram[cross[0]] = jnp.where(xh == 1, go[3].T, go[3])

    pltpu.make_async_copy(sr, sr, ss_s).wait()
    pltpu.make_async_copy(sr, sr, sg_s).wait()
    for cp in stores:
        cp.wait()
    for cp in pending:
        cp.wait_send()


def run(orb, pot, payload, kbt, lap):
    vmem = functools.partial(pltpu.VMEM)
    dma = pltpu.SemaphoreType.DMA
    f = lambda *shape: vmem(shape, F32)
    h = lambda *shape: vmem(shape, BF16)
    scratch = [
        f(4, CX, QR, ORB), f(4, CX, QR, ORB), f(4, 54, 8, ROWS), f(8, 16, ROWS), f(4, 24, NPROJ, ROWS),
        f(2, 6, NPROJ, ROWS), h(CX, ROWS, ROWS), h(CX, ROWS, ROWS), h(CX, ROWS, ROWS), h(CX, ROWS, ROWS),
        f(CX, ROWS, ORB), f(2, 24, ROWS, ORB), f(ROWS, ORB),
        f(DEGREE, 2, 6, QR, ORB), f(DEGREE, 2, 6, QR, ORB), f(3, 128, ORB),
        f(DEGREE, 3, NPROJ, ORB), f(DEGREE, 2, 3, NPROJ, ORB), h(3, 128, ORB), h(3, 128, ORB), f(CX, QR, ORB),
        f(4, CX, QR, ORB), f(4, CX, QR, ORB), f(CX, ROWS, ORB), f(CX, ROWS, ORB), f(6, ROWS, ORB), f(6, ROWS, ORB),
        f(4, 128, 128), f(3, 128, 128), f(16, 8, 128), f(15, 8, 128), f(8, 128), f(8, 128), f(16, 8, 128),
        f(4, 128, 128),
        dma((3, CH_IN)), dma((3, CH_IN)), dma((3,)), dma((3,)), dma((3,)), dma((3,)), dma((3,)), dma((3,)),
        dma((2,)), dma((2,)), dma((DEGREE, 2)), dma((DEGREE, 2)), dma((DEGREE, 2)), dma((DEGREE, 2)),
        dma((3, CH_OUT)), dma((3, CH_OUT)), dma((CH_OUT,)), dma((CH_OUT,)), dma((2,)), dma((2,)), dma((2,)), dma((2,)),
        dma((3,)), dma((3,)), dma, dma, dma((1,)), dma((1,)), dma, dma, dma((3,)), dma((3,)), dma((16,)), dma((CH_OUT,)),
    ]
    spec = pl.BlockSpec(memory_space=pltpu.VMEM)
    return pl.pallas_call(
        kernel,
        out_shape=(
            jax.ShapeDtypeStruct((CX, ROWS, ORB), F32),
            jax.ShapeDtypeStruct((4, 128, 128), F32),
        ),
        in_specs=[spec] * 5,
        out_specs=(pl.BlockSpec(memory_space=pl.ANY), spec),
        scratch_shapes=scratch,
        compiler_params=pltpu.CompilerParams(
            collective_id=0, has_side_effects=True, vmem_limit_bytes=60 * 2**20
        ),
        name="chebyshev",
    )(orb, pot, payload, kbt, lap)


def shards(orbitals, potential, projectors, atom_planes, kb_energy):
    pot = jnp.pad(potential.reshape(CX, ROWS), ((0, 4), (0, 0)))
    starts = jnp.broadcast_to(
        atom_planes[:, 0].astype(F32).reshape(2, 1, 2, 1), (2, 8, 2, 128)
    ).reshape(2, 8, ROWS)
    payload = jnp.concatenate([projectors.transpose(0, 2, 1, 3).reshape(52, 8, ROWS), starts], axis=0)
    kbt = jnp.broadcast_to(kb_energy[:, None], (8, ORB))
    filtered, gram = run(orbitals.reshape(CX, ROWS, ORB), pot, payload, kbt, jnp.asarray(plane_laplacian()))
    return filtered.reshape(orbitals.shape), gram.transpose(1, 0, 2).reshape(128, 512)


def solution(mesh):
    return jax.shard_map(
        shards,
        mesh=mesh,
        in_specs=(
            P("grid", None, None, "band"),
            P("grid", None, None),
            P("grid", None, None, None),
            P("grid", None),
            P(),
        ),
        out_specs=(P("grid", None, None, "band"), P("band", None)),
        check_vma=False,
    )
```

```python
import functools

import jax
import jax.numpy as jnp
import ml_dtypes
import numpy as np
from jax import lax
from jax.experimental import pallas as pl
from jax.experimental.pallas import tpu as pltpu
from jax.sharding import PartitionSpec as P

DEGREE = 4
CX = 12
ROWS = 256
ORB = 128
QR = 64
NPROJ = 32
CELLS = 196608
CH_IN = 3
CH_OUT = 4
WEIGHTS = (
    -5369.0 / 1800.0,
    12.0 / 7.0,
    -15.0 / 56.0,
    10.0 / 189.0,
    -1.0 / 112.0,
    2.0 / 1925.0,
    -1.0 / 16632.0,
)
HALFW = tuple(-0.5 * w for w in WEIGHTS)
LOWER = -4.0
CUTOFF = 1.0
UPPER = 16.0
F32 = jnp.float32
BF16 = jnp.bfloat16
MESH = pl.DeviceIdType.MESH


def filter_terms(degree):
    half_span = (UPPER - CUTOFF) / 2.0
    middle = (UPPER + CUTOFF) / 2.0
    sigma_now = half_span / (LOWER - middle)
    sigma_first = sigma_now
    scales = [sigma_now / half_span]
    recall = [0.0]
    for level in range(1, degree):
        sigma_next = 1.0 / (2.0 / sigma_first - sigma_now)
        scales.append(2.0 * sigma_next / half_span)
        recall.append(sigma_now * sigma_next)
        sigma_now = sigma_next
    return middle, scales, recall


def plane_laplacian():
    mat = np.zeros((16, 16, 16, 16), np.float64)
    for a in range(16):
        for b in range(16):
            for r in range(1, 7):
                for sign in (-1, 1):
                    mat[a, b, (a + sign * r) % 16, b] += HALFW[r]
                    mat[a, b, a, (b + sign * r) % 16] += HALFW[r]
    mat = mat.reshape(256, 256).astype(np.float32)
    high = mat.astype(ml_dtypes.bfloat16)
    low = (mat - high.astype(np.float32)).astype(ml_dtypes.bfloat16)
    return np.stack([high, low])


def split(value):
    high = value.astype(BF16)
    return high, (value - high.astype(F32)).astype(BF16)


def dot(a, b):
    return jnp.dot(a, b, preferred_element_type=F32)


def dot3(a_high, a_low, b_high, b_low):
    return dot(a_high, b_high) + (dot(a_high, b_low) + dot(a_low, b_high))


def dot_t(a, b):
    return lax.dot_general(a, b, (((0,), (0,)), ((), ())), preferred_element_type=F32)


def lane_block(rows):
    return lax.broadcasted_iota(jnp.int32, (rows, ORB), 1) // 32


def roll(value, blocks):
    blocks = blocks % 4
    return value if blocks == 0 else pltpu.roll(value, 32 * blocks, 1)


def transpose_blocks(parts):
    blk = lane_block(parts[0].shape[0])
    low = blk < 2
    even = (blk % 2) == 0
    a0, a1, a2, a3 = parts
    b0 = jnp.where(low, a0, roll(a2, 2))
    b2 = jnp.where(low, roll(a0, 2), a2)
    b1 = jnp.where(low, a1, roll(a3, 2))
    b3 = jnp.where(low, roll(a1, 2), a3)
    return (
        jnp.where(even, b0, roll(b1, 1)),
        jnp.where(even, roll(b0, 3), b1),
        jnp.where(even, b2, roll(b3, 1)),
        jnp.where(even, roll(b2, 3), b3),
    )


def loop(start, stop, body):
    lax.fori_loop(start, stop, lambda i, c: (body(i), c)[1], 0)


def kernel(
    orb, pot, proj, planes_ref, kb, lap, out, gram,
    flat, payload, pot_s16, x_in, r_in, pg, potg, cm, rim, chi_h, chi_l, cht_h, cht_l, pc_mat, wide, base_lv, hl,
    halo_s, halo_r, part, pc_s, pc_r, cc_h, cc_l, fix,
    x_out, r_out, filt, filt_c, xr, xr2, gb, yr, sb, sr, st, xt, tb, go,
    in_s, in_r, chi_s, chi_r, cor_s, cor_r, pot_s, pot_r, rim_s, rim_r, hal_s, hal_r, par_s, par_r,
    out_s, out_r, fc_s, fc_r, xs_s, xs_r, rl_s, rl_r, ys_s, ys_r, ss_s, ss_r, xh_s, xh_r, sg_s, sg_r, yg_s, yg_r, loc, hbm,
):
    middle, scales, recall = filter_terms(DEGREE)
    b = lax.axis_index("band")
    g = lax.axis_index("grid")
    s, y = g // 4, g % 4
    xh, c = b // 2, b % 2
    core = (2 * xh + 1 - c, g)
    across = (2 * (1 - xh) + c, g)
    cross = (2 * (1 - xh) + 1 - c, g)
    up = (b, (g + 4) % 64)
    down = (b, (g + 60) % 64)
    ypeer = [None] + [(b, 4 * s + (y + k) % 4) for k in range(1, 4)]
    speer = [None] + [(b, (g + 4 * d) % 64) for d in range(1, 16)]
    pending = []

    def rcopy(src, dst, ssem, rsem, dev):
        cp = pltpu.make_async_remote_copy(
            src_ref=src, dst_ref=dst, send_sem=ssem, recv_sem=rsem, device_id=dev, device_id_type=MESH
        )
        cp.start()
        pending.append(cp)
        return cp

    barrier = pltpu.get_barrier_semaphore()
    friends = ypeer[1:] + speer[1:] + [core, across, cross]
    for dev in friends:
        pl.semaphore_signal(barrier, inc=1, device_id=dev, device_id_type=MESH)

    for j in range(4):
        for p in range(8):
            for lh in range(2):
                flat[lh, pl.ds(128 * j + 16 * p, 13), :] = proj[j, p, :, pl.ds(128 * lh, 128)]
    for j in range(4):
        for n in range(13):
            for lh in range(2):
                payload[13 * j + n, :, pl.ds(128 * lh, 128)] = flat[lh, pl.ds(128 * j + n, 8, stride=16), :]
        payload[52 + j // 2, :, pl.ds(128 * (j % 2), 128)] = jnp.full((8, 128), planes_ref[j, 0].astype(F32))
    pot_s16[pl.ds(0, 8), :] = pot[pl.ds(0, 8), :]
    pot_s16[pl.ds(8, 8), :] = jnp.concatenate([pot[pl.ds(8, 4), :], jnp.zeros((4, ROWS), F32)], axis=0)
    p_row = lax.broadcasted_iota(jnp.int32, (8, ORB), 0)
    kbt = jnp.zeros((8, ORB), F32)
    for p in range(8):
        kbt = jnp.where(p_row == p, kb[p], kbt)
    pl.semaphore_wait(barrier, len(friends))

    half = pl.ds(27 * c, 27)
    chi_in = [None]
    pot_in = [None]
    for k in range(1, 4):
        chi_in.append(rcopy(payload.at[half], pg.at[y, half], chi_s.at[k - 1], chi_r.at[k - 1], ypeer[k]))
        pot_in.append(rcopy(pot_s16, potg.at[y], pot_s.at[k - 1], pot_r.at[k - 1], ypeer[k]))
    own_pg = pltpu.make_async_copy(payload, pg.at[y], loc.at[0])
    own_pg.start()
    own_pot = pltpu.make_async_copy(pot_s16, potg.at[y], loc.at[1])
    own_pot.start()

    span = CX // CH_IN
    orb_in = []
    orb_own = []

    def pack_in(i):
        parts = [orb[i, pl.ds(QR * q, QR), :] for q in range(4)]
        for k, value in enumerate(transpose_blocks(parts)):
            x_in[k, i] = value

    for ch in range(CH_IN):
        loop(span * ch, span * (ch + 1), pack_in)
        planes = pl.ds(span * ch, span)
        row = []
        for k in range(1, 4):
            row.append(
                rcopy(
                    x_in.at[(y + k) % 4, planes], r_in.at[y, planes],
                    in_s.at[k - 1, ch], in_r.at[k - 1, ch], ypeer[k],
                )
            )
        orb_in.append(row)
        own = pltpu.make_async_copy(x_in.at[y, planes], r_in.at[y, planes], loc.at[2 + ch])
        own.start()
        orb_own.append(own)

    for slot in range(4, 8):
        potg[slot] = jnp.zeros((16, ROWS), F32)
    own_pot.wait()
    for k in range(1, 4):
        pot_in[k].wait_recv()
    pot_t = potg[...].reshape(128, ROWS).T
    p_high = pot_t.astype(BF16)
    rest = pot_t - p_high.astype(F32)
    p_mid = rest.astype(BF16)
    p_low = (rest - p_mid.astype(F32)).astype(BF16)
    centre = 3.0 * HALFW[0] - middle
    e_row = lax.broadcasted_iota(jnp.int32, (128, ORB), 0)
    e_same = (e_row // 16) == lane_block(128)

    def spread_pot(i):
        pick = jnp.where(e_same & (e_row % 16 == i), 1.0, 0.0).astype(BF16)
        pc_mat[i] = (dot(p_high, pick) + (dot(p_mid, pick) + dot(p_low, pick))) + centre

    loop(0, CX, spread_pot)

    cor_in = [None]
    own_pg.wait()
    for k in range(1, 4):
        chi_in[k].wait_recv()
        src = (y + 4 - k) % 4
        cor_in.append(rcopy(pg.at[src, half], pg.at[src, half], cor_s.at[k - 1], cor_r.at[k - 1], core))
    for k in range(1, 4):
        cor_in[k].wait_recv()

    def place(dom):
        for j in range(4):
            start = pg[dom, 52 + j // 2, :, pl.ds(128 * (j % 2), 128)]
            bits = {}
            left = start
            for size in (8, 4, 2, 1):
                bits[size] = left >= (size - 0.5)
                left = jnp.where(bits[size], left - size, left)
            for lh in range(2):
                lanes = pl.ds(128 * lh, 128)
                zero = jnp.zeros((8, 128), F32)
                rows = [pg[dom, 13 * j + n, :, lanes] for n in range(13)]
                for size in (1, 2, 4, 8):
                    count = min(len(rows) + size, 24)
                    at = lambda n, rows=rows: rows[n] if 0 <= n < len(rows) else zero
                    rows = [jnp.where(bits[size], at(n - size), at(n)) for n in range(count)]
                for n in range(24):
                    cm[dom, n, pl.ds(8 * j, 8), lanes] = rows[n]

    loop(0, 4, place)
    rim_in = [
        rcopy(cm.at[3, pl.ds(18, 6)], rim.at[0], rim_s.at[0], rim_r.at[0], up),
        rcopy(cm.at[0, pl.ds(0, 6)], rim.at[1], rim_s.at[1], rim_r.at[1], down),
    ]
    for cp in rim_in:
        cp.wait_recv()

    def make_chi(i, beside):
        mat = jnp.concatenate([cm[d, i + 6] for d in range(4)] + beside, axis=0)
        chi_h[i], chi_l[i] = split(mat)
        cht_h[i], cht_l[i] = split(mat.T)

    loop(0, 6, lambda i: make_chi(i, [rim[0, i]] + [cm[d, i + 18] for d in range(3)]))
    loop(6, 12, lambda i: make_chi(i, [cm[d, i - 6] for d in range(1, 4)] + [rim[1, i - 6]]))

    def unpack_in(i):
        parts = [r_in[m, i] for m in range(4)]
        for q, value in enumerate(transpose_blocks(parts)):
            wide[0, 6 + i, pl.ds(QR * q, QR), :] = value
            wide[1, 6 + i, pl.ds(QR * q, QR), :] = value

    for ch in range(CH_IN):
        orb_own[ch].wait()
        for cp in orb_in[ch]:
            cp.wait_recv()
        loop(span * ch, span * (ch + 1), unpack_in)

    blk64 = lane_block(QR)
    blk32 = lane_block(NPROJ)

    def send_halo(lv, side):
        return rcopy(
            halo_s.at[lv, side], halo_r.at[lv, side], hal_s.at[lv, side], hal_r.at[lv, side], (up, down)[side]
        )

    def pack_halo(i):
        high = jnp.zeros((QR, ORB), F32)
        low = jnp.zeros((QR, ORB), F32)
        for q in range(4):
            high = jnp.where(blk64 == q, roll(wide[0, 12 + i, pl.ds(QR * q, QR), :], q - 3), high)
            low = jnp.where(blk64 == q, roll(wide[0, 6 + i, pl.ds(QR * q, QR), :], q), low)
        halo_s[0, 0, i] = high
        halo_s[0, 1, i] = low

    back_in = []
    back_own = []

    def send_out(ch):
        planes = pl.ds(3 * ch, 3)
        row = []
        for k in range(1, 4):
            row.append(
                rcopy(
                    x_out.at[(y + k) % 4, planes], r_out.at[y, planes],
                    out_s.at[k - 1, ch], out_r.at[k - 1, ch], ypeer[k],
                )
            )
        back_in.append(row)
        own = pltpu.make_async_copy(x_out.at[y, planes], r_out.at[y, planes], loc.at[8 + ch])
        own.start()
        back_own.append(own)

    loop(0, 6, pack_halo)
    halo_in = [send_halo(0, 0), send_halo(0, 1)]
    for lv in range(DEGREE):
        cur, nxt = lv % 2, 1 - lv % 2
        scale, back = scales[lv], recall[lv]
        part[...] = jnp.zeros_like(part)

        def partials(i):
            for n in range(2):
                at = i + 6 * n
                high, low = split(wide[cur, 6 + at])
                hl[i, 0, :, pl.ds(ORB * n, ORB)] = high
                hl[i, 1, :, pl.ds(ORB * n, ORB)] = low
                both = dot(chi_h[at], jnp.concatenate([high, low], axis=1))
                value = both[:, :ORB] + (both[:, ORB:] + dot(chi_l[at], high))
                part[0] += value[:128]
                part[1 + n] += value[128:]

        loop(0, 6, partials)
        for n in range(3):
            packed = jnp.zeros((NPROJ, ORB), F32)
            for d in range(4):
                packed = jnp.where(blk32 == d, part[n, pl.ds(NPROJ * d, NPROJ), :], packed)
            pc_s[lv, n] = packed
        part_in = [
            rcopy(pc_s.at[lv], pc_r.at[lv, 0], par_s.at[lv, 0], par_r.at[lv, 0], up),
            rcopy(pc_s.at[lv], pc_r.at[lv, 1], par_s.at[lv, 1], par_r.at[lv, 1], down),
        ]

        def rims(i):
            for q in range(4):
                rows = pl.ds(QR * q, QR)
                wide[cur, i, rows, :] = jnp.where(blk64 == 0, 0.0, roll(wide[cur, 12 + i, rows, :], 1))
                wide[cur, 18 + i, rows, :] = jnp.where(blk64 == 3, 0.0, roll(wide[cur, 6 + i, rows, :], 3))

        loop(0, 6, rims)

        def local(i):
            base_lv[...] = dot3(lap[0], lap[1], hl[i, 0], hl[i, 1])
            for n in range(2):
                at = i + 6 * n
                for q in range(4):
                    rows = pl.ds(QR * q, QR)
                    value = base_lv[rows, pl.ds(ORB * n, ORB)] + pc_mat[at, rows, :] * wide[cur, 6 + at, rows, :]
                    for r in range(1, 7):
                        value = value + HALFW[r] * (wide[cur, 6 + at + r, rows, :] + wide[cur, 6 + at - r, rows, :])
                    value = scale * value
                    if lv > 0:
                        value = value - back * wide[nxt, 6 + at, rows, :]
                    wide[nxt, 6 + at, rows, :] = value

        loop(0, 6, local)
        for cp in halo_in:
            cp.wait_recv()

        for i in range(6):
            low = HALFW[i + 1] * halo_r[lv, 0, 5]
            for r in range(i + 2, 7):
                low = low + HALFW[r] * halo_r[lv, 0, 6 + i - r]
            fix[i] = scale * low
            high = HALFW[6 - i] * halo_r[lv, 1, 0]
            for r in range(7 - i, 7):
                high = high + HALFW[r] * halo_r[lv, 1, i + r - 6]
            fix[6 + i] = scale * high
        for cp in part_in:
            cp.wait_recv()
        own, dn, hi = pc_s[lv, 0], pc_s[lv, 1], pc_s[lv, 2]
        corr = (
            own
            + jnp.where(blk32 == 0, roll(pc_r[lv, 0, 2], 1), roll(hi, 1))
            + jnp.where(blk32 == 3, roll(pc_r[lv, 1, 1], 3), roll(dn, 3))
        )
        corr_low = roll(pc_r[lv, 0, 0], 1) + roll(pc_r[lv, 0, 2], 2) + dn
        corr_high = roll(pc_r[lv, 1, 0], 3) + roll(pc_r[lv, 1, 1], 2) + hi
        beside_low = jnp.where(blk32 == 0, corr_low, roll(corr, 1))
        beside_high = jnp.where(blk32 == 3, corr_high, roll(corr, 3))
        energy = jnp.concatenate([kbt] * 4, axis=0) * scale
        for n, value in enumerate((corr, beside_low, beside_high)):
            high, low = split(value * energy)
            high, low = high.astype(F32), low.astype(F32)
            for d in range(4):
                rows = pl.ds(NPROJ * d, NPROJ)
                cc_h[n, rows, :] = jnp.where(blk32 == d, high, 0.0).astype(BF16)
                cc_l[n, rows, :] = jnp.where(blk32 == d, low, 0.0).astype(BF16)

        def finish(i, n, edge):
            ch = jnp.concatenate([cc_h[0], cc_h[n]], axis=0)
            cl = jnp.concatenate([cc_l[0], cc_l[n]], axis=0)
            both = dot(cht_h[i], jnp.concatenate([ch, cl], axis=1))
            value = both[:, :ORB] + (both[:, ORB:] + dot(cht_l[i], ch))
            fresh = []
            for q in range(4):
                rows = pl.ds(QR * q, QR)
                more = jnp.where(blk64 == edge, roll(fix[i], edge - q), 0.0)
                fresh.append(wide[nxt, 6 + i, rows, :] + (value[QR * q : QR * (q + 1)] + more))
            if lv == DEGREE - 1:
                for k, moved in enumerate(transpose_blocks(fresh)):
                    x_out[k, i] = moved
            else:
                packed = jnp.zeros((QR, ORB), F32)
                for q in range(4):
                    wide[nxt, 6 + i, pl.ds(QR * q, QR), :] = fresh[q]
                    packed = jnp.where(blk64 == q, roll(fresh[q], q - edge), packed)
                halo_s[lv + 1, 1 - edge // 3, i - 2 * edge] = packed

        def finish_two(i, n, edge):
            finish(i, n, edge)
            finish(i + 1, n, edge)

        if lv == DEGREE - 1:
            for ch in range(CH_OUT):
                n, edge = (1, 0) if ch < 2 else (2, 3)
                for i in range(3):
                    finish(3 * ch + i, n, edge)
                send_out(ch)
        else:
            loop(0, 3, lambda i: finish_two(6 + 2 * i, 2, 3))
            upward = send_halo(lv + 1, 0)
            loop(0, 3, lambda i: finish_two(2 * i, 1, 0))
            halo_in = [upward, send_halo(lv + 1, 1)]

    def unpack_out(i):
        parts = [r_out[m, i] for m in range(4)]
        for q, value in enumerate(transpose_blocks(parts)):
            filt[i, pl.ds(QR * q, QR), :] = value

    gb[...] = jnp.zeros_like(gb)

    def gram_step(slot, lhs, rhs):
        a_high, a_low = split(lhs)
        parts = [split(value) for value in rhs]
        r_high = jnp.concatenate([p[0] for p in parts], axis=1)
        r_low = jnp.concatenate([p[1] for p in parts], axis=1)
        value = dot_t(a_high, r_high) + (dot_t(a_high, r_low) + dot_t(a_low, r_high))
        gb[slot] += value[:, :128]
        gb[slot + 1] += value[:, 128:]

    fc_in = []
    x_recv = []
    stores = []
    relay = []
    keep = pl.ds(128 * xh, 128)
    give = pl.ds(128 * (1 - xh), 128)

    def near(ch):
        fc_in[ch].wait_recv()
        loop(3 * ch, 3 * ch + 3, lambda i: gram_step(0, filt[i], [filt[i], filt_c[i]]))

    def pass_on(ch):
        x_recv[ch].wait_recv()
        planes = pl.ds(3 * ch, 3)
        relay.append(rcopy(xr.at[planes], xr2.at[planes], rl_s.at[ch], rl_r.at[ch], core))

    def flat_rows(ref, i, rows):
        return ref[pl.ds(3 * i, 3), rows, :].reshape(3 * 128, ORB)

    for ch in range(CH_OUT):
        back_own[ch].wait()
        for cp in back_in[ch]:
            cp.wait_recv()
        loop(3 * ch, 3 * ch + 3, unpack_out)
        planes = pl.ds(3 * ch, 3)
        x_recv.append(rcopy(filt.at[planes, give], xr.at[planes], xs_s.at[ch], xs_r.at[ch], across))
        fc_in.append(rcopy(filt.at[planes], filt_c.at[planes], fc_s.at[ch], fc_r.at[ch], core))
        store = pltpu.make_async_copy(filt.at[planes], out.at[planes], hbm.at[ch])
        store.start()
        stores.append(store)
        if ch > 0:
            near(ch - 1)
        if ch > 1:
            pass_on(ch - 2)
    near(CH_OUT - 1)
    every = pl.ds(0, 128)
    for ch in range(CH_OUT):
        if ch < 2:
            pass_on(ch + 2)
        relay[ch].wait_recv()
        gram_step(2, flat_rows(filt, ch, keep), [flat_rows(xr, ch, every), flat_rows(xr2, ch, every)])
    for n in (2, 3):
        gb[n] = jnp.where(xh == 1, gb[n].T, gb[n])

    y_in = []
    for k in range(1, 4):
        y_in.append(rcopy(gb.at[(y + k) % 4], yr.at[k - 1], ys_s.at[k - 1], ys_r.at[k - 1], ypeer[k]))
    for cp in y_in:
        cp.wait_recv()
    sb[...] = (gb[y] + (yr[0] + (yr[1] + yr[2]))).reshape(16, 8, 128)
    for d in range(1, 16):
        cp = pltpu.make_async_remote_copy(
            src_ref=sb.at[(s + d) % 16], dst_ref=sr.at[d - 1], send_sem=ss_s, recv_sem=ss_r,
            device_id=speer[d], device_id_type=MESH,
        )
        cp.start()
    pltpu.make_async_copy(sr, sr, ss_r).wait()
    tile = sb[s]
    for d in range(15):
        tile = tile + sr[d]
    st[...] = tile
    partner = (2 * (1 - xh) + (c + y // 3 * (1 - 2 * c)), g)
    xh_in = rcopy(st, xt, xh_s.at[0], xh_r.at[0], partner)
    xh_in.wait_recv()
    tb[s] = tile + jnp.where(y >= 2, xt[...], 0.0)
    for d in range(1, 16):
        cp = pltpu.make_async_remote_copy(
            src_ref=tb.at[s], dst_ref=tb.at[s], send_sem=sg_s, recv_sem=sg_r,
            device_id=speer[d], device_id_type=MESH,
        )
        cp.start()
    pltpu.make_async_copy(sr, sr, sg_r).wait()
    go[y] = tb[...].reshape(128, 128) * (1.0 / CELLS)
    yg_in = []
    for k in range(1, 4):
        yg_in.append(rcopy(go.at[y], go.at[y], yg_s.at[k - 1], yg_r.at[k - 1], ypeer[k]))
    for cp in yg_in:
        cp.wait_recv()
    for n, dev in enumerate((b, core[0], across[0], cross[0])):
        value = go[n] if n < 2 else jnp.where(xh == 1, go[n].T, go[n])
        gram[:, pl.ds(pl.multiple_of(128 * dev, 128), 128)] = value

    pltpu.make_async_copy(sr, sr, ss_s).wait()
    pltpu.make_async_copy(sr, sr, sg_s).wait()
    for cp in stores:
        cp.wait()
    for cp in pending:
        cp.wait_send()


def run(orb, pot, proj, planes_ref, kb, lap):
    vmem = functools.partial(pltpu.VMEM)
    dma = pltpu.SemaphoreType.DMA
    f = lambda *shape: vmem(shape, F32)
    h = lambda *shape: vmem(shape, BF16)
    scratch = [
        f(2, 512, 128), f(54, 8, ROWS), f(16, ROWS),
        f(4, CX, QR, ORB), f(4, CX, QR, ORB), f(4, 54, 8, ROWS), f(8, 16, ROWS), f(4, 24, NPROJ, ROWS),
        f(2, 6, NPROJ, ROWS), h(CX, ROWS, ROWS), h(CX, ROWS, ROWS), h(CX, ROWS, ROWS), h(CX, ROWS, ROWS),
        f(CX, ROWS, ORB), f(2, 24, ROWS, ORB), f(ROWS, 2 * ORB), h(6, 2, ROWS, 2 * ORB),
        f(DEGREE, 2, 6, QR, ORB), f(DEGREE, 2, 6, QR, ORB), f(3, 128, ORB),
        f(DEGREE, 3, NPROJ, ORB), f(DEGREE, 2, 3, NPROJ, ORB), h(3, 128, ORB), h(3, 128, ORB), f(CX, QR, ORB),
        f(4, CX, QR, ORB), f(4, CX, QR, ORB), f(CX, ROWS, ORB), f(CX, ROWS, ORB), f(CX, 128, ORB), f(CX, 128, ORB),
        f(4, 128, 128), f(3, 128, 128), f(16, 8, 128), f(15, 8, 128), f(8, 128), f(8, 128), f(16, 8, 128),
        f(4, 128, 128),
        dma((3, CH_IN)), dma((3, CH_IN)), dma((3,)), dma((3,)), dma((3,)), dma((3,)), dma((3,)), dma((3,)),
        dma((2,)), dma((2,)), dma((DEGREE, 2)), dma((DEGREE, 2)), dma((DEGREE, 2)), dma((DEGREE, 2)),
        dma((3, CH_OUT)), dma((3, CH_OUT)), dma((CH_OUT,)), dma((CH_OUT,)),
        dma((CH_OUT,)), dma((CH_OUT,)), dma((CH_OUT,)), dma((CH_OUT,)),
        dma((3,)), dma((3,)), dma, dma, dma((1,)), dma((1,)), dma, dma, dma((3,)), dma((3,)), dma((16,)), dma((CH_OUT,)),
    ]
    spec = pl.BlockSpec(memory_space=pltpu.VMEM)
    smem = pl.BlockSpec(memory_space=pltpu.SMEM)
    return pl.pallas_call(
        kernel,
        out_shape=(
            jax.ShapeDtypeStruct((CX, ROWS, ORB), F32),
            jax.ShapeDtypeStruct((128, 512), F32),
        ),
        in_specs=[spec, spec, spec, smem, smem, spec],
        out_specs=(pl.BlockSpec(memory_space=pl.ANY), spec),
        scratch_shapes=scratch,
        compiler_params=pltpu.CompilerParams(
            collective_id=0, has_side_effects=True, vmem_limit_bytes=60 * 2**20
        ),
        name="chebyshev",
    )(orb, pot, proj, planes_ref, kb, lap)


def shards(orbitals, potential, projectors, atom_planes, kb_energy):
    filtered, gram = run(
        orbitals.reshape(CX, ROWS, ORB), potential.reshape(CX, ROWS), projectors, atom_planes, kb_energy,
        jnp.asarray(plane_laplacian()),
    )
    return filtered.reshape(orbitals.shape), gram


def solution(mesh):
    return jax.shard_map(
        shards,
        mesh=mesh,
        in_specs=(
            P("grid", None, None, "band"),
            P("grid", None, None),
            P("grid", None, None, None),
            P("grid", None),
            P(),
        ),
        out_specs=(P("grid", None, None, "band"), P("band", None)),
        check_vma=False,
    )
```

```python
import functools

import jax
import jax.numpy as jnp
import ml_dtypes
import numpy as np
from jax import lax
from jax.experimental import pallas as pl
from jax.experimental.pallas import tpu as pltpu
from jax.sharding import PartitionSpec as P

DEGREE = 4
CX = 12
ROWS = 256
ORB = 128
QR = 64
NPROJ = 32
CELLS = 196608
CH_IN = 3
CH_OUT = 6
PART_OUT = CX // CH_OUT
WEIGHTS = (
    -5369.0 / 1800.0,
    12.0 / 7.0,
    -15.0 / 56.0,
    10.0 / 189.0,
    -1.0 / 112.0,
    2.0 / 1925.0,
    -1.0 / 16632.0,
)
HALFW = tuple(-0.5 * w for w in WEIGHTS)
LOWER = -4.0
CUTOFF = 1.0
UPPER = 16.0
F32 = jnp.float32
BF16 = jnp.bfloat16
MESH = pl.DeviceIdType.MESH


def filter_terms(degree):
    half_span = (UPPER - CUTOFF) / 2.0
    middle = (UPPER + CUTOFF) / 2.0
    sigma_now = half_span / (LOWER - middle)
    sigma_first = sigma_now
    scales = [sigma_now / half_span]
    recall = [0.0]
    for level in range(1, degree):
        sigma_next = 1.0 / (2.0 / sigma_first - sigma_now)
        scales.append(2.0 * sigma_next / half_span)
        recall.append(sigma_now * sigma_next)
        sigma_now = sigma_next
    return middle, scales, recall


def plane_laplacian():
    mat = np.zeros((16, 16, 16, 16), np.float64)
    for a in range(16):
        for b in range(16):
            for r in range(1, 7):
                for sign in (-1, 1):
                    mat[a, b, (a + sign * r) % 16, b] += HALFW[r]
                    mat[a, b, a, (b + sign * r) % 16] += HALFW[r]
    mat = mat.reshape(256, 256).astype(np.float32)
    high = mat.astype(ml_dtypes.bfloat16)
    low = (mat - high.astype(np.float32)).astype(ml_dtypes.bfloat16)
    return np.stack([high, low])


def split(value):
    high = value.astype(BF16)
    return high, (value - high.astype(F32)).astype(BF16)


def split3(value):
    high = value.astype(BF16)
    rest = value - high.astype(F32)
    mid = rest.astype(BF16)
    return high, mid, (rest - mid.astype(F32)).astype(BF16)


def dot(a, b):
    return jnp.dot(a, b, preferred_element_type=F32)


def dot3(a_high, a_low, b_high, b_low):
    return dot(a_high, b_high) + (dot(a_high, b_low) + dot(a_low, b_high))


def dot_t(a, b):
    return lax.dot_general(a, b, (((0,), (0,)), ((), ())), preferred_element_type=F32)


def lane_block(rows):
    return lax.broadcasted_iota(jnp.int32, (rows, ORB), 1) // 32


def roll(value, blocks):
    blocks = blocks % 4
    return value if blocks == 0 else pltpu.roll(value, 32 * blocks, 1)


def transpose_blocks(parts):
    blk = lane_block(parts[0].shape[0])
    low = blk < 2
    even = (blk % 2) == 0
    a0, a1, a2, a3 = parts
    b0 = jnp.where(low, a0, roll(a2, 2))
    b2 = jnp.where(low, roll(a0, 2), a2)
    b1 = jnp.where(low, a1, roll(a3, 2))
    b3 = jnp.where(low, roll(a1, 2), a3)
    return (
        jnp.where(even, b0, roll(b1, 1)),
        jnp.where(even, roll(b0, 3), b1),
        jnp.where(even, b2, roll(b3, 1)),
        jnp.where(even, roll(b2, 3), b3),
    )


def loop(start, stop, body):
    lax.fori_loop(start, stop, lambda i, c: (body(i), c)[1], 0)


def kernel(
    orb, pot, proj, planes_ref, kb, lap, out, gram,
    payload, pot_s16, x_in, r_in, pg, potg, cm, rim, chi_h, chi_l, cht_h, cht_l, pc_mat, wide, base_lv, hl,
    halo_s, halo_r, part, pc_s, pc_r, cc_h, cc_l, fix,
    x_out, r_out, filt, filt_c, xr, xr2, gb, z_r, zs, y_r, ws, x1_r, x2_r, go,
    in_s, in_r, chi_s, chi_r, acr_s, acr_r, cor_s, cor_r, pot_s, pot_r, rim_s, rim_r, hal_s, hal_r, par_s, par_r,
    out_s, out_r, fc_s, fc_r, xs_s, xs_r, rl_s, rl_r, za_s, za_r, zb_s, zb_r, ye_s, ye_r, xe_s, xe_r, zg_s, zg_r, loc, hbm,
):
    middle, scales, recall = filter_terms(DEGREE)
    b = lax.axis_index("band")
    g = lax.axis_index("grid")
    s, y = g // 4, g % 4
    z, xl = s % 8, s // 8
    xh, c = b // 2, b % 2
    core = (2 * xh + 1 - c, g)
    across = (2 * (1 - xh) + c, g)
    cross = (2 * (1 - xh) + 1 - c, g)
    other = (g + 32) % 64
    up = (b, (g + 4) % 64)
    down = (b, (g + 60) % 64)
    ypeer = [None] + [(b, 4 * s + (y + k) % 4) for k in range(1, 4)]
    zpeer = [None] + [(b, 32 * xl + 4 * ((z + k) % 8) + y) for k in range(1, 8)]
    xpeers = [(b, other), across, (across[0], other), cross, (cross[0], other)]
    pending = []

    def rcopy(src, dst, ssem, rsem, dev):
        cp = pltpu.make_async_remote_copy(
            src_ref=src, dst_ref=dst, send_sem=ssem, recv_sem=rsem, device_id=dev, device_id_type=MESH
        )
        cp.start()
        pending.append(cp)
        return cp

    barrier = pltpu.get_barrier_semaphore()
    friends = ypeer[1:] + zpeer[1:] + xpeers + [up, down, core]
    for dev in friends:
        pl.semaphore_signal(barrier, inc=1, device_id=dev, device_id_type=MESH)

    payload[pl.ds(0, 52)] = proj[...]
    payload[pl.ds(54, 2)] = jnp.zeros((2, 8, ROWS), F32)
    for j in range(4):
        payload[52 + j // 2, :, pl.ds(128 * (j % 2), 128)] = jnp.full((8, 128), planes_ref[j, 0].astype(F32))
    p_pick = (
        lax.broadcasted_iota(jnp.int32, (16, ROWS), 1) % 16 == lax.broadcasted_iota(jnp.int32, (16, ROWS), 0)
    )
    p_pick = jnp.where(p_pick, 1.0, 0.0).astype(BF16)
    p_high, p_mid, p_low = split3(pot[...].reshape(16 * CX, 16))
    wide_pot = dot(p_high, p_pick) + (dot(p_mid, p_pick) + dot(p_low, p_pick))
    p_mine = (
        lax.broadcasted_iota(jnp.int32, (16 * CX, ROWS), 1) // 16
        == lax.broadcasted_iota(jnp.int32, (16 * CX, ROWS), 0) % 16
    )
    rows_pot = jnp.sum(jnp.where(p_mine, wide_pot, 0.0).reshape(CX, 16, ROWS), axis=1)
    pot_s16[...] = jnp.concatenate([rows_pot, jnp.zeros((4, ROWS), F32)], axis=0)
    p_row = lax.broadcasted_iota(jnp.int32, (8, ORB), 0)
    kbt = jnp.zeros((8, ORB), F32)
    for p in range(8):
        kbt = jnp.where(p_row == p, kb[p], kbt)
    pl.semaphore_wait(barrier, len(friends))

    mine = pl.ds(14 * b, 14)
    theirs = pl.ds(14 * across[0], 14)
    chi_in = [None]
    pot_in = [None]
    for k in range(1, 4):
        chi_in.append(rcopy(payload.at[mine], pg.at[y, mine], chi_s.at[k - 1], chi_r.at[k - 1], ypeer[k]))
        pot_in.append(rcopy(pot_s16, potg.at[y], pot_s.at[k - 1], pot_r.at[k - 1], ypeer[k]))
    own_pg = pltpu.make_async_copy(payload, pg.at[y], loc.at[0])
    own_pg.start()
    own_pot = pltpu.make_async_copy(pot_s16, potg.at[y], loc.at[1])
    own_pot.start()

    span = CX // CH_IN
    orb_in = []
    orb_own = []

    def pack_in(i):
        parts = [orb[i, pl.ds(QR * q, QR), :] for q in range(4)]
        for k, value in enumerate(transpose_blocks(parts)):
            x_in[k, i] = value

    for ch in range(CH_IN):
        loop(span * ch, span * (ch + 1), pack_in)
        planes = pl.ds(span * ch, span)
        row = []
        for k in range(1, 4):
            row.append(
                rcopy(
                    x_in.at[(y + k) % 4, planes], r_in.at[y, planes],
                    in_s.at[k - 1, ch], in_r.at[k - 1, ch], ypeer[k],
                )
            )
        orb_in.append(row)
        own = pltpu.make_async_copy(x_in.at[y, planes], r_in.at[y, planes], loc.at[2 + ch])
        own.start()
        orb_own.append(own)

    for slot in range(4, 8):
        potg[slot] = jnp.zeros((16, ROWS), F32)
    own_pot.wait()
    for k in range(1, 4):
        pot_in[k].wait_recv()
    pot_t = potg[...].reshape(128, ROWS).T
    p_high, p_mid, p_low = split3(pot_t)
    centre = 3.0 * HALFW[0] - middle
    e_row = lax.broadcasted_iota(jnp.int32, (128, ORB), 0)
    e_same = (e_row // 16) == lane_block(128)

    def spread_pot(i):
        pick = jnp.where(e_same & (e_row % 16 == i), 1.0, 0.0).astype(BF16)
        pc_mat[i] = (dot(p_high, pick) + (dot(p_mid, pick) + dot(p_low, pick))) + centre

    loop(0, CX, spread_pot)

    acr_in = []
    cor_in = []
    own_pg.wait()
    for k in range(1, 4):
        chi_in[k].wait_recv()
        src = (y + 4 - k) % 4
        acr_in.append(rcopy(pg.at[src, mine], pg.at[src, mine], acr_s.at[k - 1], acr_r.at[k - 1], across))
        cor_in.append(rcopy(pg.at[src, mine], pg.at[src, mine], cor_s.at[0, k - 1], cor_r.at[0, k - 1], core))
    for k in range(1, 4):
        acr_in[k - 1].wait_recv()
        src = (y + 4 - k) % 4
        cor_in.append(rcopy(pg.at[src, theirs], pg.at[src, theirs], cor_s.at[1, k - 1], cor_r.at[1, k - 1], core))
    for cp in cor_in:
        cp.wait_recv()

    def place(dom):
        for j in range(4):
            start = pg[dom, 52 + j // 2, :, pl.ds(128 * (j % 2), 128)]
            bits = {}
            left = start
            for size in (8, 4, 2, 1):
                bits[size] = left >= (size - 0.5)
                left = jnp.where(bits[size], left - size, left)
            for lh in range(2):
                lanes = pl.ds(128 * lh, 128)
                zero = jnp.zeros((8, 128), F32)
                rows = [pg[dom, 13 * j + n, :, lanes] for n in range(13)]
                for size in (1, 2, 4, 8):
                    count = min(len(rows) + size, 24)
                    at = lambda n, rows=rows: rows[n] if 0 <= n < len(rows) else zero
                    rows = [jnp.where(bits[size], at(n - size), at(n)) for n in range(count)]
                for n in range(24):
                    cm[dom, n, pl.ds(8 * j, 8), lanes] = rows[n]

    loop(0, 4, place)
    rim_in = [
        rcopy(cm.at[3, pl.ds(18, 6)], rim.at[0], rim_s.at[0], rim_r.at[0], up),
        rcopy(cm.at[0, pl.ds(0, 6)], rim.at[1], rim_s.at[1], rim_r.at[1], down),
    ]

    def make_chi(i, first, blocks):
        mat = jnp.concatenate(blocks, axis=0)
        rows = pl.ds(first, 128)
        chi_h[i, rows, :], chi_l[i, rows, :] = split(mat)
        cht_h[i, :, rows], cht_l[i, :, rows] = split(mat.T)

    loop(0, CX, lambda i: make_chi(i, 0, [cm[d, i + 6] for d in range(4)]))

    def unpack_in(i):
        parts = [r_in[m, i] for m in range(4)]
        for q, value in enumerate(transpose_blocks(parts)):
            wide[0, 6 + i, pl.ds(QR * q, QR), :] = value
            wide[1, 6 + i, pl.ds(QR * q, QR), :] = value

    for ch in range(CH_IN):
        orb_own[ch].wait()
        for cp in orb_in[ch]:
            cp.wait_recv()
        loop(span * ch, span * (ch + 1), unpack_in)

    blk64 = lane_block(QR)
    blk32 = lane_block(NPROJ)

    def send_halo(lv, side):
        return rcopy(
            halo_s.at[lv, side], halo_r.at[lv, side], hal_s.at[lv, side], hal_r.at[lv, side], (up, down)[side]
        )

    def pack_halo(i):
        high = jnp.zeros((QR, ORB), F32)
        low = jnp.zeros((QR, ORB), F32)
        for q in range(4):
            high = jnp.where(blk64 == q, roll(wide[0, 12 + i, pl.ds(QR * q, QR), :], q - 3), high)
            low = jnp.where(blk64 == q, roll(wide[0, 6 + i, pl.ds(QR * q, QR), :], q), low)
        halo_s[0, 0, i] = high
        halo_s[0, 1, i] = low

    back_in = []
    back_own = []

    def send_out(ch):
        planes = pl.ds(PART_OUT * ch, PART_OUT)
        row = []
        for k in range(1, 4):
            row.append(
                rcopy(
                    x_out.at[(y + k) % 4, planes], r_out.at[y, planes],
                    out_s.at[k - 1, ch], out_r.at[k - 1, ch], ypeer[k],
                )
            )
        back_in.append(row)
        own = pltpu.make_async_copy(x_out.at[y, planes], r_out.at[y, planes], loc.at[8 + ch])
        own.start()
        back_own.append(own)

    loop(0, 6, pack_halo)
    halo_in = [send_halo(0, 0), send_halo(0, 1)]
    for cp in rim_in:
        cp.wait_recv()
    loop(0, 6, lambda i: make_chi(i, 128, [rim[0, i]] + [cm[d, i + 18] for d in range(3)]))
    loop(6, 12, lambda i: make_chi(i, 128, [cm[d, i - 6] for d in range(1, 4)] + [rim[1, i - 6]]))
    for lv in range(DEGREE):
        cur, nxt = lv % 2, 1 - lv % 2
        scale, back = scales[lv], recall[lv]
        part[...] = jnp.zeros_like(part)

        def partials(i):
            for n in range(2):
                at = i + 6 * n
                high, low = split(wide[cur, 6 + at])
                hl[i, 0, :, pl.ds(ORB * n, ORB)] = high
                hl[i, 1, :, pl.ds(ORB * n, ORB)] = low
                both = dot(chi_h[at], jnp.concatenate([high, low], axis=1))
                value = both[:, :ORB] + (both[:, ORB:] + dot(chi_l[at], high))
                part[0] += value[:128]
                part[1 + n] += value[128:]

        loop(0, 6, partials)
        for n in range(3):
            packed = jnp.zeros((NPROJ, ORB), F32)
            for d in range(4):
                packed = jnp.where(blk32 == d, part[n, pl.ds(NPROJ * d, NPROJ), :], packed)
            pc_s[lv, n] = packed
        part_in = [
            rcopy(pc_s.at[lv], pc_r.at[lv, 0], par_s.at[lv, 0], par_r.at[lv, 0], up),
            rcopy(pc_s.at[lv], pc_r.at[lv, 1], par_s.at[lv, 1], par_r.at[lv, 1], down),
        ]

        def rims(i):
            for q in range(4):
                rows = pl.ds(QR * q, QR)
                wide[cur, i, rows, :] = jnp.where(blk64 == 0, 0.0, roll(wide[cur, 12 + i, rows, :], 1))
                wide[cur, 18 + i, rows, :] = jnp.where(blk64 == 3, 0.0, roll(wide[cur, 6 + i, rows, :], 3))

        loop(0, 6, rims)

        def local(i):
            base_lv[...] = dot3(lap[0], lap[1], hl[i, 0], hl[i, 1])
            for n in range(2):
                at = i + 6 * n
                for q in range(4):
                    rows = pl.ds(QR * q, QR)
                    value = base_lv[rows, pl.ds(ORB * n, ORB)] + pc_mat[at, rows, :] * wide[cur, 6 + at, rows, :]
                    for r in range(1, 7):
                        value = value + HALFW[r] * (wide[cur, 6 + at + r, rows, :] + wide[cur, 6 + at - r, rows, :])
                    value = scale * value
                    if lv > 0:
                        value = value - back * wide[nxt, 6 + at, rows, :]
                    wide[nxt, 6 + at, rows, :] = value

        loop(0, 6, local)
        for cp in halo_in:
            cp.wait_recv()

        for i in range(6):
            low = HALFW[i + 1] * halo_r[lv, 0, 5]
            for r in range(i + 2, 7):
                low = low + HALFW[r] * halo_r[lv, 0, 6 + i - r]
            fix[i] = scale * low
            high = HALFW[6 - i] * halo_r[lv, 1, 0]
            for r in range(7 - i, 7):
                high = high + HALFW[r] * halo_r[lv, 1, i + r - 6]
            fix[6 + i] = scale * high
        for cp in part_in:
            cp.wait_recv()
        own, dn, hi = pc_s[lv, 0], pc_s[lv, 1], pc_s[lv, 2]
        corr = (
            own
            + jnp.where(blk32 == 0, roll(pc_r[lv, 0, 2], 1), roll(hi, 1))
            + jnp.where(blk32 == 3, roll(pc_r[lv, 1, 1], 3), roll(dn, 3))
        )
        corr_low = roll(pc_r[lv, 0, 0], 1) + roll(pc_r[lv, 0, 2], 2) + dn
        corr_high = roll(pc_r[lv, 1, 0], 3) + roll(pc_r[lv, 1, 1], 2) + hi
        beside_low = jnp.where(blk32 == 0, corr_low, roll(corr, 1))
        beside_high = jnp.where(blk32 == 3, corr_high, roll(corr, 3))
        energy = jnp.concatenate([kbt] * 4, axis=0) * scale
        for n, value in enumerate((corr, beside_low, beside_high)):
            high, low = split(value * energy)
            high, low = high.astype(F32), low.astype(F32)
            for d in range(4):
                rows = pl.ds(NPROJ * d, NPROJ)
                cc_h[n, rows, :] = jnp.where(blk32 == d, high, 0.0).astype(BF16)
                cc_l[n, rows, :] = jnp.where(blk32 == d, low, 0.0).astype(BF16)

        def finish(i, n, edge):
            ch = jnp.concatenate([cc_h[0], cc_h[n]], axis=0)
            cl = jnp.concatenate([cc_l[0], cc_l[n]], axis=0)
            both = dot(cht_h[i], jnp.concatenate([ch, cl], axis=1))
            value = both[:, :ORB] + (both[:, ORB:] + dot(cht_l[i], ch))
            fresh = []
            for q in range(4):
                rows = pl.ds(QR * q, QR)
                more = jnp.where(blk64 == edge, roll(fix[i], edge - q), 0.0)
                fresh.append(wide[nxt, 6 + i, rows, :] + (value[QR * q : QR * (q + 1)] + more))
            if lv == DEGREE - 1:
                for k, moved in enumerate(transpose_blocks(fresh)):
                    x_out[k, i] = moved
            else:
                packed = jnp.zeros((QR, ORB), F32)
                for q in range(4):
                    wide[nxt, 6 + i, pl.ds(QR * q, QR), :] = fresh[q]
                    packed = jnp.where(blk64 == q, roll(fresh[q], q - edge), packed)
                halo_s[lv + 1, 1 - edge // 3, i - 2 * edge] = packed

        def finish_two(i, n, edge):
            finish(i, n, edge)
            finish(i + 1, n, edge)

        if lv == DEGREE - 1:
            for ch in range(CH_OUT):
                n, edge = (1, 0) if 2 * ch < CH_OUT else (2, 3)
                for i in range(PART_OUT):
                    finish(PART_OUT * ch + i, n, edge)
                send_out(ch)
        else:
            loop(0, 3, lambda i: finish_two(6 + 2 * i, 2, 3))
            upward = send_halo(lv + 1, 0)
            loop(0, 3, lambda i: finish_two(2 * i, 1, 0))
            halo_in = [upward, send_halo(lv + 1, 1)]

    def unpack_out(i):
        parts = [r_out[m, i] for m in range(4)]
        for q, value in enumerate(transpose_blocks(parts)):
            filt[i, pl.ds(QR * q, QR), :] = value

    gb[...] = jnp.zeros_like(gb)

    def gram_step(slot, lhs, rhs):
        a_high, a_low = split(lhs)
        parts = [split(value) for value in rhs]
        r_high = jnp.concatenate([p[0] for p in parts], axis=1)
        r_low = jnp.concatenate([p[1] for p in parts], axis=1)
        value = dot_t(a_high, r_high) + (dot_t(a_high, r_low) + dot_t(a_low, r_high))
        gb[slot] += value[:, :128]
        gb[slot + 1] += value[:, 128:]

    fc_in = []
    x_recv = []
    stores = []
    relay = []
    keep = pl.ds(128 * xh, 128)
    give = pl.ds(128 * (1 - xh), 128)

    def near(ch):
        fc_in[ch].wait_recv()
        loop(PART_OUT * ch, PART_OUT * (ch + 1), lambda i: gram_step(0, filt[i], [filt[i], filt_c[i]]))

    def pass_on(ch):
        x_recv[ch].wait_recv()
        planes = pl.ds(PART_OUT * ch, PART_OUT)
        relay.append(rcopy(xr.at[planes], xr2.at[planes], rl_s.at[ch], rl_r.at[ch], core))

    def flat_rows(ref, i, rows):
        return ref[pl.ds(PART_OUT * i, PART_OUT), rows, :].reshape(PART_OUT * 128, ORB)

    for ch in range(CH_OUT):
        back_own[ch].wait()
        for cp in back_in[ch]:
            cp.wait_recv()
        loop(PART_OUT * ch, PART_OUT * (ch + 1), unpack_out)
        planes = pl.ds(PART_OUT * ch, PART_OUT)
        x_recv.append(rcopy(filt.at[planes, give], xr.at[planes], xs_s.at[ch], xs_r.at[ch], across))
        fc_in.append(rcopy(filt.at[planes], filt_c.at[planes], fc_s.at[ch], fc_r.at[ch], core))
        store = pltpu.make_async_copy(filt.at[planes], out.at[planes], hbm.at[ch])
        store.start()
        stores.append(store)
        if ch > 0:
            near(ch - 1)
        if ch > 2:
            pass_on(ch - 3)
    near(CH_OUT - 1)

    def to_z(first, ssem, rsem):
        for k in range(1, 8):
            pltpu.make_async_remote_copy(
                src_ref=gb.at[pl.ds(first, 2), pl.ds(16 * ((z + k) % 8), 16)], dst_ref=z_r.at[first // 2, k - 1],
                send_sem=ssem, recv_sem=rsem, device_id=zpeer[k], device_id_type=MESH,
            ).start()

    every = pl.ds(0, 128)
    for ch in range(CH_OUT):
        if ch + 3 < CH_OUT:
            pass_on(ch + 3)
        if ch == 0:
            to_z(0, za_s, za_r)
        relay[ch].wait_recv()
        gram_step(2, flat_rows(filt, ch, keep), [flat_rows(xr, ch, every), flat_rows(xr2, ch, every)])
    for n in (2, 3):
        gb[n] = jnp.where(xh == 1, gb[n].T, gb[n])

    to_z(2, zb_s, zb_r)
    tile = pl.ds(16 * z, 16)
    for n, sem in ((0, za_r), (1, zb_r)):
        pltpu.make_async_copy(z_r.at[n], z_r.at[n], sem).wait()
        value = gb[pl.ds(2 * n, 2), tile, :]
        for k in range(7):
            value = value + z_r[n, k]
        zs[pl.ds(2 * n, 2)] = value
    y_in = [rcopy(zs, y_r.at[k - 1], ye_s.at[k - 1], ye_r.at[k - 1], ypeer[k]) for k in range(1, 4)]
    for cp in y_in:
        cp.wait_recv()
    ws[...] = zs[...] + (y_r[0] + (y_r[1] + y_r[2]))
    x_in2 = [rcopy(ws, x1_r, xe_s.at[0], xe_r.at[0], xpeers[0])]
    for k in range(1, 5):
        x_in2.append(rcopy(ws.at[2 + (k - 1) // 2], x2_r.at[k - 1], xe_s.at[k], xe_r.at[k], xpeers[k]))
    for cp in x_in2:
        cp.wait_recv()
    pair = ws[...] + x1_r[...]
    go[pl.ds(0, 2), tile, :] = pair[:2] * (1.0 / CELLS)
    go[2, tile, :] = (pair[2] + (x2_r[0] + x2_r[1])) * (1.0 / CELLS)
    go[3, tile, :] = (pair[3] + (x2_r[2] + x2_r[3])) * (1.0 / CELLS)
    for k in range(1, 8):
        pltpu.make_async_remote_copy(
            src_ref=go.at[:, tile], dst_ref=go.at[:, tile], send_sem=zg_s, recv_sem=zg_r,
            device_id=zpeer[k], device_id_type=MESH,
        ).start()
    pltpu.make_async_copy(z_r, z_r, zg_r).wait()
    for n, dev in enumerate((b, core[0], across[0], cross[0])):
        value = go[n] if n < 2 else jnp.where(xh == 1, go[n].T, go[n])
        gram[:, pl.ds(pl.multiple_of(128 * dev, 128), 128)] = value

    pltpu.make_async_copy(z_r.at[0], z_r.at[0], za_s).wait()
    pltpu.make_async_copy(z_r.at[1], z_r.at[1], zb_s).wait()
    pltpu.make_async_copy(z_r, z_r, zg_s).wait()
    for cp in stores:
        cp.wait()
    for cp in pending:
        cp.wait_send()


def run(orb, pot, proj, planes_ref, kb, lap):
    vmem = functools.partial(pltpu.VMEM)
    dma = pltpu.SemaphoreType.DMA
    f = lambda *shape: vmem(shape, F32)
    h = lambda *shape: vmem(shape, BF16)
    scratch = [
        f(56, 8, ROWS), f(16, ROWS),
        f(4, CX, QR, ORB), f(4, CX, QR, ORB), f(4, 56, 8, ROWS), f(8, 16, ROWS), f(4, 24, NPROJ, ROWS),
        f(2, 6, NPROJ, ROWS), h(CX, ROWS, ROWS), h(CX, ROWS, ROWS), h(CX, ROWS, ROWS), h(CX, ROWS, ROWS),
        f(CX, ROWS, ORB), f(2, 24, ROWS, ORB), f(ROWS, 2 * ORB), h(6, 2, ROWS, 2 * ORB),
        f(DEGREE, 2, 6, QR, ORB), f(DEGREE, 2, 6, QR, ORB), f(3, 128, ORB),
        f(DEGREE, 3, NPROJ, ORB), f(DEGREE, 2, 3, NPROJ, ORB), h(3, 128, ORB), h(3, 128, ORB), f(CX, QR, ORB),
        f(4, CX, QR, ORB), f(4, CX, QR, ORB), f(CX, ROWS, ORB), f(CX, ROWS, ORB), f(CX, 128, ORB), f(CX, 128, ORB),
        f(4, 128, 128), f(2, 7, 2, 16, 128), f(4, 16, 128), f(3, 4, 16, 128), f(4, 16, 128), f(4, 16, 128),
        f(4, 16, 128), f(4, 128, 128),
        dma((3, CH_IN)), dma((3, CH_IN)), dma((3,)), dma((3,)), dma((3,)), dma((3,)), dma((2, 3)), dma((2, 3)),
        dma((3,)), dma((3,)),
        dma((2,)), dma((2,)), dma((DEGREE, 2)), dma((DEGREE, 2)), dma((DEGREE, 2)), dma((DEGREE, 2)),
        dma((3, CH_OUT)), dma((3, CH_OUT)), dma((CH_OUT,)), dma((CH_OUT,)),
        dma((CH_OUT,)), dma((CH_OUT,)), dma((CH_OUT,)), dma((CH_OUT,)),
        dma, dma, dma, dma, dma((3,)), dma((3,)), dma((5,)), dma((5,)), dma, dma, dma((16,)), dma((CH_OUT,)),
    ]
    spec = pl.BlockSpec(memory_space=pltpu.VMEM)
    smem = pl.BlockSpec(memory_space=pltpu.SMEM)
    return pl.pallas_call(
        kernel,
        out_shape=(
            jax.ShapeDtypeStruct((CX, ROWS, ORB), F32),
            jax.ShapeDtypeStruct((128, 512), F32),
        ),
        in_specs=[spec, spec, spec, smem, smem, spec],
        out_specs=(pl.BlockSpec(memory_space=pl.ANY), spec),
        scratch_shapes=scratch,
        compiler_params=pltpu.CompilerParams(
            collective_id=0, has_side_effects=True, vmem_limit_bytes=60 * 2**20
        ),
        name="chebyshev",
    )(orb, pot, proj, planes_ref, kb, lap)


def shards(orbitals, potential, projectors, atom_planes, kb_energy):
    filtered, gram = run(
        orbitals.reshape(CX, ROWS, ORB), potential, projectors.transpose(0, 2, 1, 3).reshape(52, 8, ROWS),
        atom_planes, kb_energy,
        jnp.asarray(plane_laplacian()),
    )
    return filtered.reshape(orbitals.shape), gram


def solution(mesh):
    return jax.shard_map(
        shards,
        mesh=mesh,
        in_specs=(
            P("grid", None, None, "band"),
            P("grid", None, None),
            P("grid", None, None, None),
            P("grid", None),
            P(),
        ),
        out_specs=(P("grid", None, None, "band"), P("band", None)),
        check_vma=False,
    )
```

```python
import functools

import jax
import jax.numpy as jnp
import ml_dtypes
import numpy as np
from jax import lax
from jax.experimental import pallas as pl
from jax.experimental.pallas import tpu as pltpu
from jax.sharding import PartitionSpec as P

DEGREE = 4
CX = 12
ROWS = 256
ORB = 128
QR = 64
NPROJ = 32
CELLS = 196608
CH_IN = 3
CH_OUT = 6
PART_OUT = CX // CH_OUT
WEIGHTS = (
    -5369.0 / 1800.0,
    12.0 / 7.0,
    -15.0 / 56.0,
    10.0 / 189.0,
    -1.0 / 112.0,
    2.0 / 1925.0,
    -1.0 / 16632.0,
)
HALFW = tuple(-0.5 * w for w in WEIGHTS)
LOWER = -4.0
CUTOFF = 1.0
UPPER = 16.0
F32 = jnp.float32
BF16 = jnp.bfloat16
MESH = pl.DeviceIdType.MESH


def filter_terms(degree):
    half_span = (UPPER - CUTOFF) / 2.0
    middle = (UPPER + CUTOFF) / 2.0
    sigma_now = half_span / (LOWER - middle)
    sigma_first = sigma_now
    scales = [sigma_now / half_span]
    recall = [0.0]
    for level in range(1, degree):
        sigma_next = 1.0 / (2.0 / sigma_first - sigma_now)
        scales.append(2.0 * sigma_next / half_span)
        recall.append(sigma_now * sigma_next)
        sigma_now = sigma_next
    return middle, scales, recall


def plane_laplacian():
    mat = np.zeros((16, 16, 16, 16), np.float64)
    for a in range(16):
        for b in range(16):
            for r in range(1, 7):
                for sign in (-1, 1):
                    mat[a, b, (a + sign * r) % 16, b] += HALFW[r]
                    mat[a, b, a, (b + sign * r) % 16] += HALFW[r]
    mat = mat.reshape(256, 256).astype(np.float32)
    high = mat.astype(ml_dtypes.bfloat16)
    low = (mat - high.astype(np.float32)).astype(ml_dtypes.bfloat16)
    return np.stack([high, low])


def split(value):
    high = value.astype(BF16)
    return high, (value - high.astype(F32)).astype(BF16)


def split3(value):
    high = value.astype(BF16)
    rest = value - high.astype(F32)
    mid = rest.astype(BF16)
    return high, mid, (rest - mid.astype(F32)).astype(BF16)


def dot(a, b):
    return jnp.dot(a, b, preferred_element_type=F32)


def dot3(a_high, a_low, b_high, b_low):
    return dot(a_high, b_high) + (dot(a_high, b_low) + dot(a_low, b_high))


def dot_t(a, b):
    return lax.dot_general(a, b, (((0,), (0,)), ((), ())), preferred_element_type=F32)


def lane_block(rows):
    return lax.broadcasted_iota(jnp.int32, (rows, ORB), 1) // 32


def roll(value, blocks):
    blocks = blocks % 4
    return value if blocks == 0 else pltpu.roll(value, 32 * blocks, 1)


def transpose_blocks(parts):
    blk = lane_block(parts[0].shape[0])
    low = blk < 2
    even = (blk % 2) == 0
    a0, a1, a2, a3 = parts
    b0 = jnp.where(low, a0, roll(a2, 2))
    b2 = jnp.where(low, roll(a0, 2), a2)
    b1 = jnp.where(low, a1, roll(a3, 2))
    b3 = jnp.where(low, roll(a1, 2), a3)
    return (
        jnp.where(even, b0, roll(b1, 1)),
        jnp.where(even, roll(b0, 3), b1),
        jnp.where(even, b2, roll(b3, 1)),
        jnp.where(even, roll(b2, 3), b3),
    )


def loop(start, stop, body, unroll=1):
    lax.fori_loop(start, stop, lambda i, c: (body(i), c)[1], 0, unroll=unroll)


def kernel(
    orb, pot, proj, planes_ref, kb, lap, out, gram,
    payload, pot_s16, x_in, r_in, pg, potg, cm, rim, chi_h, chi_l, cht_h, cht_l, pc_mat, wide, base_lv, hl,
    halo_s, halo_r, part, pc_s, pc_r, cc_h, cc_l, fix,
    x_out, r_out, filt, filt_c, xr, xr2, gb, z_r, zs, y_r, ws, x1_r, x2_r, go,
    in_s, in_r, chi_s, chi_r, acr_s, acr_r, cor_s, cor_r, pot_s, pot_r, rim_s, rim_r, hal_s, hal_r, par_s, par_r,
    out_s, out_r, fc_s, fc_r, xs_s, xs_r, rl_s, rl_r, za_s, za_r, zb_s, zb_r, ye_s, ye_r, xe_s, xe_r, zg_s, zg_r, loc, hbm,
):
    middle, scales, recall = filter_terms(DEGREE)
    b = lax.axis_index("band")
    g = lax.axis_index("grid")
    s, y = g // 4, g % 4
    z, xl = s % 8, s // 8
    xh, c = b // 2, b % 2
    core = (2 * xh + 1 - c, g)
    across = (2 * (1 - xh) + c, g)
    cross = (2 * (1 - xh) + 1 - c, g)
    other = (g + 32) % 64
    up = (b, (g + 4) % 64)
    down = (b, (g + 60) % 64)
    ypeer = [None] + [(b, 4 * s + (y + k) % 4) for k in range(1, 4)]
    zpeer = [None] + [(b, 32 * xl + 4 * ((z + k) % 8) + y) for k in range(1, 8)]
    xpeers = [(b, other), across, (across[0], other), cross, (cross[0], other)]
    pending = []

    def rcopy(src, dst, ssem, rsem, dev):
        cp = pltpu.make_async_remote_copy(
            src_ref=src, dst_ref=dst, send_sem=ssem, recv_sem=rsem, device_id=dev, device_id_type=MESH
        )
        cp.start()
        pending.append(cp)
        return cp

    barrier = pltpu.get_barrier_semaphore()
    friends = ypeer[1:] + zpeer[1:] + xpeers + [up, down, core]
    for dev in friends:
        pl.semaphore_signal(barrier, inc=1, device_id=dev, device_id_type=MESH)

    payload[pl.ds(0, 52)] = proj[...]
    payload[pl.ds(54, 2)] = jnp.zeros((2, 8, ROWS), F32)
    for j in range(4):
        payload[52 + j // 2, :, pl.ds(128 * (j % 2), 128)] = jnp.full((8, 128), planes_ref[j, 0].astype(F32))
    p_pick = (
        lax.broadcasted_iota(jnp.int32, (16, ROWS), 1) % 16 == lax.broadcasted_iota(jnp.int32, (16, ROWS), 0)
    )
    p_pick = jnp.where(p_pick, 1.0, 0.0).astype(BF16)
    p_high, p_mid, p_low = split3(pot[...].reshape(16 * CX, 16))
    wide_pot = dot(p_high, p_pick) + (dot(p_mid, p_pick) + dot(p_low, p_pick))
    p_mine = (
        lax.broadcasted_iota(jnp.int32, (16 * CX, ROWS), 1) // 16
        == lax.broadcasted_iota(jnp.int32, (16 * CX, ROWS), 0) % 16
    )
    rows_pot = jnp.sum(jnp.where(p_mine, wide_pot, 0.0).reshape(CX, 16, ROWS), axis=1)
    pot_s16[...] = jnp.concatenate([rows_pot, jnp.zeros((4, ROWS), F32)], axis=0)
    p_row = lax.broadcasted_iota(jnp.int32, (8, ORB), 0)
    kbt = jnp.zeros((8, ORB), F32)
    for p in range(8):
        kbt = jnp.where(p_row == p, kb[p], kbt)
    def pack_in(i):
        parts = [orb[i, pl.ds(QR * q, QR), :] for q in range(4)]
        for k, value in enumerate(transpose_blocks(parts)):
            x_in[k, i] = value

    loop(0, CX, pack_in, 2)
    pl.semaphore_wait(barrier, len(friends))

    mine = pl.ds(14 * b, 14)
    theirs = pl.ds(14 * across[0], 14)
    chi_in = [None]
    pot_in = [None]
    for k in range(1, 4):
        chi_in.append(rcopy(payload.at[mine], pg.at[y, mine], chi_s.at[k - 1], chi_r.at[k - 1], ypeer[k]))
        pot_in.append(rcopy(pot_s16, potg.at[y], pot_s.at[k - 1], pot_r.at[k - 1], ypeer[k]))
    own_pg = pltpu.make_async_copy(payload, pg.at[y], loc.at[0])
    own_pg.start()
    own_pot = pltpu.make_async_copy(pot_s16, potg.at[y], loc.at[1])
    own_pot.start()

    span = CX // CH_IN
    orb_in = []
    orb_own = []

    for ch in range(CH_IN):
        planes = pl.ds(span * ch, span)
        row = []
        for k in range(1, 4):
            row.append(
                rcopy(
                    x_in.at[(y + k) % 4, planes], r_in.at[y, planes],
                    in_s.at[k - 1, ch], in_r.at[k - 1, ch], ypeer[k],
                )
            )
        orb_in.append(row)
        own = pltpu.make_async_copy(x_in.at[y, planes], r_in.at[y, planes], loc.at[2 + ch])
        own.start()
        orb_own.append(own)

    acr_in = []
    cor_in = []
    own_pg.wait()
    for k in range(1, 4):
        chi_in[k].wait_recv()
        src = (y + 4 - k) % 4
        acr_in.append(rcopy(pg.at[src, mine], pg.at[src, mine], acr_s.at[k - 1], acr_r.at[k - 1], across))
        cor_in.append(rcopy(pg.at[src, mine], pg.at[src, mine], cor_s.at[0, k - 1], cor_r.at[0, k - 1], core))
    for slot in range(4, 8):
        potg[slot] = jnp.zeros((16, ROWS), F32)
    own_pot.wait()
    for k in range(1, 4):
        pot_in[k].wait_recv()
    pot_t = potg[...].reshape(128, ROWS).T
    p_high, p_mid, p_low = split3(pot_t)
    centre = 3.0 * HALFW[0] - middle
    e_row = lax.broadcasted_iota(jnp.int32, (128, ORB), 0)
    e_same = (e_row // 16) == lane_block(128)

    def spread_pot(i):
        pick = jnp.where(e_same & (e_row % 16 == i), 1.0, 0.0).astype(BF16)
        pc_mat[i] = (dot(p_high, pick) + (dot(p_mid, pick) + dot(p_low, pick))) + centre

    loop(0, CX, spread_pot)

    for k in range(1, 4):
        acr_in[k - 1].wait_recv()
        src = (y + 4 - k) % 4
        cor_in.append(rcopy(pg.at[src, theirs], pg.at[src, theirs], cor_s.at[1, k - 1], cor_r.at[1, k - 1], core))
    for cp in cor_in:
        cp.wait_recv()

    def place(dom):
        for j in range(4):
            start = pg[dom, 52 + j // 2, :, pl.ds(128 * (j % 2), 128)]
            bits = {}
            left = start
            for size in (8, 4, 2, 1):
                bits[size] = left >= (size - 0.5)
                left = jnp.where(bits[size], left - size, left)
            for lh in range(2):
                lanes = pl.ds(128 * lh, 128)
                zero = jnp.zeros((8, 128), F32)
                rows = [pg[dom, 13 * j + n, :, lanes] for n in range(13)]
                for size in (1, 2, 4, 8):
                    count = min(len(rows) + size, 24)
                    at = lambda n, rows=rows: rows[n] if 0 <= n < len(rows) else zero
                    rows = [jnp.where(bits[size], at(n - size), at(n)) for n in range(count)]
                for n in range(24):
                    cm[dom, n, pl.ds(8 * j, 8), lanes] = rows[n]

    loop(0, 4, place)
    rim_in = [
        rcopy(cm.at[3, pl.ds(18, 6)], rim.at[0], rim_s.at[0], rim_r.at[0], up),
        rcopy(cm.at[0, pl.ds(0, 6)], rim.at[1], rim_s.at[1], rim_r.at[1], down),
    ]

    def make_chi(i, first, blocks):
        mat = jnp.concatenate(blocks, axis=0)
        rows = pl.ds(first, 128)
        chi_h[i, rows, :], chi_l[i, rows, :] = split(mat)
        cht_h[i, :, rows], cht_l[i, :, rows] = split(mat.T)

    loop(0, CX, lambda i: make_chi(i, 0, [cm[d, i + 6] for d in range(4)]))

    for cp in rim_in:
        cp.wait_recv()
    loop(0, 6, lambda i: make_chi(i, 128, [rim[0, i]] + [cm[d, i + 18] for d in range(3)]))
    loop(6, 12, lambda i: make_chi(i, 128, [cm[d, i - 6] for d in range(1, 4)] + [rim[1, i - 6]]))

    def unpack_in(i):
        parts = [r_in[m, i] for m in range(4)]
        for q, value in enumerate(transpose_blocks(parts)):
            wide[0, 6 + i, pl.ds(QR * q, QR), :] = value
            wide[1, 6 + i, pl.ds(QR * q, QR), :] = value

    for ch in range(CH_IN):
        orb_own[ch].wait()
        for cp in orb_in[ch]:
            cp.wait_recv()
        loop(span * ch, span * (ch + 1), unpack_in)

    blk64 = lane_block(QR)
    blk32 = lane_block(NPROJ)

    def send_halo(lv, side, piece):
        planes = (pl.ds(0, 2), pl.ds(2, 4))[piece]
        return rcopy(
            halo_s.at[lv, side, planes], halo_r.at[lv, side, planes],
            hal_s.at[lv, side, piece], hal_r.at[lv, side, piece], (up, down)[side],
        )

    def pack_halo(i):
        high = jnp.zeros((QR, ORB), F32)
        low = jnp.zeros((QR, ORB), F32)
        for q in range(4):
            high = jnp.where(blk64 == q, roll(wide[0, 12 + i, pl.ds(QR * q, QR), :], q - 3), high)
            low = jnp.where(blk64 == q, roll(wide[0, 6 + i, pl.ds(QR * q, QR), :], q), low)
        halo_s[0, 0, i] = high
        halo_s[0, 1, i] = low

    back_in = []
    back_own = []

    def send_out(ch):
        planes = pl.ds(PART_OUT * ch, PART_OUT)
        row = []
        for k in range(1, 4):
            row.append(
                rcopy(
                    x_out.at[(y + k) % 4, planes], r_out.at[y, planes],
                    out_s.at[k - 1, ch], out_r.at[k - 1, ch], ypeer[k],
                )
            )
        back_in.append(row)
        own = pltpu.make_async_copy(x_out.at[y, planes], r_out.at[y, planes], loc.at[8 + ch])
        own.start()
        back_own.append(own)

    loop(0, 6, pack_halo)
    halo_in = [send_halo(0, 0, 0), send_halo(0, 1, 0)]

    def mended(buf, i, edge):
        groups = []
        for q in range(4):
            more = jnp.where(blk64 == edge, roll(fix[i], edge - q), 0.0)
            groups.append(wide[buf, 6 + i, pl.ds(QR * q, QR), :] + more)
        return groups

    for lv in range(DEGREE):
        cur, nxt = lv % 2, 1 - lv % 2
        scale, back = scales[lv], recall[lv]
        part[...] = jnp.zeros_like(part)

        def partials(i):
            for n in range(2):
                at = i + 6 * n
                if lv == 0:
                    value = wide[cur, 6 + at]
                else:
                    value = jnp.concatenate(mended(cur, at, 3 * n), axis=0)
                    wide[cur, 6 + at] = value
                high, low = split(value)
                hl[i, 0, :, pl.ds(ORB * n, ORB)] = high
                hl[i, 1, :, pl.ds(ORB * n, ORB)] = low
                both = dot(chi_h[at], jnp.concatenate([high, low], axis=1))
                value = both[:, :ORB] + (both[:, ORB:] + dot(chi_l[at], high))
                part[0] += value[:128]
                part[1 + n] += value[128:]

        loop(0, 6, partials, 6)
        for n in range(3):
            packed = jnp.zeros((NPROJ, ORB), F32)
            for d in range(4):
                packed = jnp.where(blk32 == d, part[n, pl.ds(NPROJ * d, NPROJ), :], packed)
            pc_s[lv, n] = packed
        own, dn, hi = pc_s[lv, 0], pc_s[lv, 1], pc_s[lv, 2]
        pc_s[lv, 3] = roll(hi, 2) + jnp.where(blk32 == 0, roll(own, 1), 0.0)
        pc_s[lv, 4] = roll(dn, 2) + jnp.where(blk32 == 3, roll(own, 3), 0.0)
        part_in = [
            rcopy(pc_s.at[lv, 3], pc_r.at[lv, 0], par_s.at[lv, 0], par_r.at[lv, 0], up),
            rcopy(pc_s.at[lv, 4], pc_r.at[lv, 1], par_s.at[lv, 1], par_r.at[lv, 1], down),
        ]
        halo_rest = [send_halo(lv, 0, 1), send_halo(lv, 1, 1)]

        def rims(i):
            for q in range(4):
                rows = pl.ds(QR * q, QR)
                wide[cur, i, rows, :] = jnp.where(blk64 == 0, 0.0, roll(wide[cur, 12 + i, rows, :], 1))
                wide[cur, 18 + i, rows, :] = jnp.where(blk64 == 3, 0.0, roll(wide[cur, 6 + i, rows, :], 3))

        loop(0, 6, rims)

        def local(i):
            base_lv[...] = dot3(lap[0], lap[1], hl[i, 0], hl[i, 1])
            for n in range(2):
                at = i + 6 * n
                for q in range(4):
                    rows = pl.ds(QR * q, QR)
                    value = base_lv[rows, pl.ds(ORB * n, ORB)] + pc_mat[at, rows, :] * wide[cur, 6 + at, rows, :]
                    for r in range(1, 7):
                        value = value + HALFW[r] * (wide[cur, 6 + at + r, rows, :] + wide[cur, 6 + at - r, rows, :])
                    value = scale * value
                    if lv > 0:
                        value = value - back * wide[nxt, 6 + at, rows, :]
                    wide[nxt, 6 + at, rows, :] = value

        loop(0, 6, local, 6)
        for cp in part_in:
            cp.wait_recv()
        own, dn, hi = pc_s[lv, 0], pc_s[lv, 1], pc_s[lv, 2]
        below, above = pc_r[lv, 0], pc_r[lv, 1]
        corr = (
            own
            + jnp.where(blk32 == 0, roll(below, 3), roll(hi, 1))
            + jnp.where(blk32 == 3, roll(above, 1), roll(dn, 3))
        )
        corr_low = below + dn
        corr_high = above + hi
        beside_low = jnp.where(blk32 == 0, corr_low, roll(corr, 1))
        beside_high = jnp.where(blk32 == 3, corr_high, roll(corr, 3))
        energy = jnp.concatenate([kbt] * 4, axis=0) * scale
        for n, value in enumerate((corr, beside_low, beside_high)):
            high, low = split(value * energy)
            high, low = high.astype(F32), low.astype(F32)
            for d in range(4):
                rows = pl.ds(NPROJ * d, NPROJ)
                cc_h[n, rows, :] = jnp.where(blk32 == d, high, 0.0).astype(BF16)
                cc_l[n, rows, :] = jnp.where(blk32 == d, low, 0.0).astype(BF16)

        def spread(i, n, edge):
            ch = jnp.concatenate([cc_h[0], cc_h[n]], axis=0)
            cl = jnp.concatenate([cc_l[0], cc_l[n]], axis=0)
            both = dot(cht_h[i], jnp.concatenate([ch, cl], axis=1))
            value = both[:, :ORB] + (both[:, ORB:] + dot(cht_l[i], ch))
            packed = jnp.zeros((QR, ORB), F32)
            for q in range(4):
                rows = pl.ds(QR * q, QR)
                fresh = wide[nxt, 6 + i, rows, :] + value[QR * q : QR * (q + 1)]
                wide[nxt, 6 + i, rows, :] = fresh
                packed = jnp.where(blk64 == q, roll(fresh, q - edge), packed)
            if lv + 1 < DEGREE:
                halo_s[lv + 1, 1 - edge // 3, i - 2 * edge] = packed

        def spread_both(i):
            spread(i, 1, 0)
            spread(6 + i, 2, 3)

        loop(0, 6, spread_both, 6)

        halo_in[0].wait_recv()
        halo_rest[0].wait_recv()
        for i in range(6):
            low = HALFW[i + 1] * halo_r[lv, 0, 5]
            for r in range(i + 2, 7):
                low = low + HALFW[r] * halo_r[lv, 0, 6 + i - r]
            low = scale * low
            fix[i] = low
            if lv + 1 < DEGREE:
                halo_s[lv + 1, 1, i] = halo_s[lv + 1, 1, i] + low
        if lv + 1 < DEGREE:
            downward = send_halo(lv + 1, 1, 0)
        halo_in[1].wait_recv()
        halo_rest[1].wait_recv()
        for i in range(6):
            high = HALFW[6 - i] * halo_r[lv, 1, 0]
            for r in range(7 - i, 7):
                high = high + HALFW[r] * halo_r[lv, 1, i + r - 6]
            high = scale * high
            fix[6 + i] = high
            if lv + 1 < DEGREE:
                halo_s[lv + 1, 0, i] = halo_s[lv + 1, 0, i] + high
        if lv + 1 < DEGREE:
            halo_in = [send_halo(lv + 1, 0, 0), downward]

    for ch in range(CH_OUT):
        for i in range(PART_OUT * ch, PART_OUT * (ch + 1)):
            for k, moved in enumerate(transpose_blocks(mended(DEGREE % 2, i, 3 * (i // 6)))):
                x_out[k, i] = moved
        send_out(ch)

    def unpack_out(i):
        parts = [r_out[m, i] for m in range(4)]
        for q, value in enumerate(transpose_blocks(parts)):
            filt[i, pl.ds(QR * q, QR), :] = value

    gb[...] = jnp.zeros_like(gb)

    def gram_step(slot, lhs, rhs):
        a_high, a_low = split(lhs)
        parts = [split(value) for value in rhs]
        r_high = jnp.concatenate([p[0] for p in parts], axis=1)
        r_low = jnp.concatenate([p[1] for p in parts], axis=1)
        value = dot_t(a_high, r_high) + (dot_t(a_high, r_low) + dot_t(a_low, r_high))
        gb[slot] += value[:, :128]
        gb[slot + 1] += value[:, 128:]

    fc_in = []
    x_recv = []
    stores = []
    relay = []
    keep = pl.ds(128 * xh, 128)
    give = pl.ds(128 * (1 - xh), 128)

    def near(ch):
        fc_in[ch].wait_recv()
        loop(PART_OUT * ch, PART_OUT * (ch + 1), lambda i: gram_step(0, filt[i], [filt[i], filt_c[i]]), PART_OUT)

    def pass_on(ch):
        x_recv[ch].wait_recv()
        planes = pl.ds(PART_OUT * ch, PART_OUT)
        relay.append(rcopy(xr.at[planes], xr2.at[planes], rl_s.at[ch], rl_r.at[ch], core))

    def flat_rows(ref, i, rows):
        return ref[pl.ds(PART_OUT * i, PART_OUT), rows, :].reshape(PART_OUT * 128, ORB)

    for ch in range(CH_OUT):
        back_own[ch].wait()
        for cp in back_in[ch]:
            cp.wait_recv()
        loop(PART_OUT * ch, PART_OUT * (ch + 1), unpack_out, PART_OUT)
        planes = pl.ds(PART_OUT * ch, PART_OUT)
        x_recv.append(rcopy(filt.at[planes, give], xr.at[planes], xs_s.at[ch], xs_r.at[ch], across))
        fc_in.append(rcopy(filt.at[planes], filt_c.at[planes], fc_s.at[ch], fc_r.at[ch], core))
        store = pltpu.make_async_copy(filt.at[planes], out.at[planes], hbm.at[ch])
        store.start()
        stores.append(store)
        if ch > 0:
            near(ch - 1)
        if ch > 2:
            pass_on(ch - 3)
    near(CH_OUT - 1)

    def to_z(first, ssem, rsem):
        for k in range(1, 8):
            pltpu.make_async_remote_copy(
                src_ref=gb.at[pl.ds(first, 2), pl.ds(16 * ((z + k) % 8), 16)], dst_ref=z_r.at[first // 2, k - 1],
                send_sem=ssem, recv_sem=rsem, device_id=zpeer[k], device_id_type=MESH,
            ).start()

    every = pl.ds(0, 128)
    for ch in range(CH_OUT):
        if ch + 3 < CH_OUT:
            pass_on(ch + 3)
        if ch == 0:
            to_z(0, za_s, za_r)
        relay[ch].wait_recv()
        gram_step(2, flat_rows(filt, ch, keep), [flat_rows(xr, ch, every), flat_rows(xr2, ch, every)])
    for n in (2, 3):
        gb[n] = jnp.where(xh == 1, gb[n].T, gb[n])

    to_z(2, zb_s, zb_r)
    tile = pl.ds(16 * z, 16)
    for n, sem in ((0, za_r), (1, zb_r)):
        pltpu.make_async_copy(z_r.at[n], z_r.at[n], sem).wait()
        value = gb[pl.ds(2 * n, 2), tile, :]
        for k in range(7):
            value = value + z_r[n, k]
        zs[pl.ds(2 * n, 2)] = value
    y_in = [rcopy(zs, y_r.at[k - 1], ye_s.at[k - 1], ye_r.at[k - 1], ypeer[k]) for k in range(1, 4)]
    for cp in y_in:
        cp.wait_recv()
    ws[...] = zs[...] + (y_r[0] + (y_r[1] + y_r[2]))
    x_in2 = [rcopy(ws, x1_r, xe_s.at[0], xe_r.at[0], xpeers[0])]
    for k in range(1, 5):
        x_in2.append(rcopy(ws.at[2 + (k - 1) // 2], x2_r.at[k - 1], xe_s.at[k], xe_r.at[k], xpeers[k]))
    for cp in x_in2:
        cp.wait_recv()
    pair = ws[...] + x1_r[...]
    go[pl.ds(0, 2), tile, :] = pair[:2] * (1.0 / CELLS)
    go[2, tile, :] = (pair[2] + (x2_r[0] + x2_r[1])) * (1.0 / CELLS)
    go[3, tile, :] = (pair[3] + (x2_r[2] + x2_r[3])) * (1.0 / CELLS)
    for k in range(1, 8):
        pltpu.make_async_remote_copy(
            src_ref=go.at[:, tile], dst_ref=go.at[:, tile], send_sem=zg_s, recv_sem=zg_r,
            device_id=zpeer[k], device_id_type=MESH,
        ).start()
    pltpu.make_async_copy(z_r, z_r, zg_r).wait()
    for n, dev in enumerate((b, core[0], across[0], cross[0])):
        value = go[n] if n < 2 else jnp.where(xh == 1, go[n].T, go[n])
        gram[:, pl.ds(pl.multiple_of(128 * dev, 128), 128)] = value

    pltpu.make_async_copy(z_r.at[0], z_r.at[0], za_s).wait()
    pltpu.make_async_copy(z_r.at[1], z_r.at[1], zb_s).wait()
    pltpu.make_async_copy(z_r, z_r, zg_s).wait()
    for cp in stores:
        cp.wait()
    for cp in pending:
        cp.wait_send()


def run(orb, pot, proj, planes_ref, kb, lap):
    vmem = functools.partial(pltpu.VMEM)
    dma = pltpu.SemaphoreType.DMA
    f = lambda *shape: vmem(shape, F32)
    h = lambda *shape: vmem(shape, BF16)
    scratch = [
        f(56, 8, ROWS), f(16, ROWS),
        f(4, CX, QR, ORB), f(4, CX, QR, ORB), f(4, 56, 8, ROWS), f(8, 16, ROWS), f(4, 24, NPROJ, ROWS),
        f(2, 6, NPROJ, ROWS), h(CX, ROWS, ROWS), h(CX, ROWS, ROWS), h(CX, ROWS, ROWS), h(CX, ROWS, ROWS),
        f(CX, ROWS, ORB), f(2, 24, ROWS, ORB), f(ROWS, 2 * ORB), h(6, 2, ROWS, 2 * ORB),
        f(DEGREE, 2, 6, QR, ORB), f(DEGREE, 2, 6, QR, ORB), f(3, 128, ORB),
        f(DEGREE, 5, NPROJ, ORB), f(DEGREE, 2, NPROJ, ORB), h(3, 128, ORB), h(3, 128, ORB), f(CX, QR, ORB),
        f(4, CX, QR, ORB), f(4, CX, QR, ORB), f(CX, ROWS, ORB), f(CX, ROWS, ORB), f(CX, 128, ORB), f(CX, 128, ORB),
        f(4, 128, 128), f(2, 7, 2, 16, 128), f(4, 16, 128), f(3, 4, 16, 128), f(4, 16, 128), f(4, 16, 128),
        f(4, 16, 128), f(4, 128, 128),
        dma((3, CH_IN)), dma((3, CH_IN)), dma((3,)), dma((3,)), dma((3,)), dma((3,)), dma((2, 3)), dma((2, 3)),
        dma((3,)), dma((3,)),
        dma((2,)), dma((2,)), dma((DEGREE, 2, 2)), dma((DEGREE, 2, 2)), dma((DEGREE, 2)), dma((DEGREE, 2)),
        dma((3, CH_OUT)), dma((3, CH_OUT)), dma((CH_OUT,)), dma((CH_OUT,)),
        dma((CH_OUT,)), dma((CH_OUT,)), dma((CH_OUT,)), dma((CH_OUT,)),
        dma, dma, dma, dma, dma((3,)), dma((3,)), dma((5,)), dma((5,)), dma, dma, dma((16,)), dma((CH_OUT,)),
    ]
    spec = pl.BlockSpec(memory_space=pltpu.VMEM)
    smem = pl.BlockSpec(memory_space=pltpu.SMEM)
    return pl.pallas_call(
        kernel,
        out_shape=(
            jax.ShapeDtypeStruct((CX, ROWS, ORB), F32),
            jax.ShapeDtypeStruct((128, 512), F32),
        ),
        in_specs=[spec, spec, spec, smem, smem, spec],
        out_specs=(pl.BlockSpec(memory_space=pl.ANY), spec),
        scratch_shapes=scratch,
        compiler_params=pltpu.CompilerParams(
            collective_id=0, has_side_effects=True, vmem_limit_bytes=60 * 2**20
        ),
        name="chebyshev",
    )(orb, pot, proj, planes_ref, kb, lap)


def shards(orbitals, potential, projectors, atom_planes, kb_energy):
    filtered, gram = run(
        orbitals.reshape(CX, ROWS, ORB), potential, projectors.transpose(0, 2, 1, 3).reshape(52, 8, ROWS),
        atom_planes, kb_energy,
        jnp.asarray(plane_laplacian()),
    )
    return filtered.reshape(orbitals.shape), gram


def solution(mesh):
    return jax.shard_map(
        shards,
        mesh=mesh,
        in_specs=(
            P("grid", None, None, "band"),
            P("grid", None, None),
            P("grid", None, None, None),
            P("grid", None),
            P(),
        ),
        out_specs=(P("grid", None, None, "band"), P("band", None)),
        check_vma=False,
    )
```

```python
import functools

import jax
import jax.numpy as jnp
import ml_dtypes
import numpy as np
from jax import lax
from jax.experimental import pallas as pl
from jax.experimental.pallas import tpu as pltpu
from jax.sharding import PartitionSpec as P

DEGREE = 4
CX = 12
ROWS = 256
ORB = 128
QR = 64
NPROJ = 32
CELLS = 196608
CH_IN = 3
CH_OUT = 6
PART_OUT = CX // CH_OUT
WEIGHTS = (
    -5369.0 / 1800.0,
    12.0 / 7.0,
    -15.0 / 56.0,
    10.0 / 189.0,
    -1.0 / 112.0,
    2.0 / 1925.0,
    -1.0 / 16632.0,
)
HALFW = tuple(-0.5 * w for w in WEIGHTS)
LOWER = -4.0
CUTOFF = 1.0
UPPER = 16.0
F32 = jnp.float32
BF16 = jnp.bfloat16
MESH = pl.DeviceIdType.MESH


def filter_terms(degree):
    half_span = (UPPER - CUTOFF) / 2.0
    middle = (UPPER + CUTOFF) / 2.0
    sigma_now = half_span / (LOWER - middle)
    sigma_first = sigma_now
    scales = [sigma_now / half_span]
    recall = [0.0]
    for level in range(1, degree):
        sigma_next = 1.0 / (2.0 / sigma_first - sigma_now)
        scales.append(2.0 * sigma_next / half_span)
        recall.append(sigma_now * sigma_next)
        sigma_now = sigma_next
    return middle, scales, recall


def plane_laplacian():
    mat = np.zeros((16, 16, 16, 16), np.float64)
    for a in range(16):
        for b in range(16):
            for r in range(1, 7):
                for sign in (-1, 1):
                    mat[a, b, (a + sign * r) % 16, b] += HALFW[r]
                    mat[a, b, a, (b + sign * r) % 16] += HALFW[r]
    mat = mat.reshape(256, 256).astype(np.float32)
    high = mat.astype(ml_dtypes.bfloat16)
    low = (mat - high.astype(np.float32)).astype(ml_dtypes.bfloat16)
    return np.stack([high, low])


def split(value):
    high = value.astype(BF16)
    return high, (value - high.astype(F32)).astype(BF16)


def split3(value):
    high = value.astype(BF16)
    rest = value - high.astype(F32)
    mid = rest.astype(BF16)
    return high, mid, (rest - mid.astype(F32)).astype(BF16)


def dot(a, b):
    return jnp.dot(a, b, preferred_element_type=F32)


def dot3(a_high, a_low, b_high, b_low):
    return dot(a_high, b_high) + (dot(a_high, b_low) + dot(a_low, b_high))


def dot_t(a, b):
    return lax.dot_general(a, b, (((0,), (0,)), ((), ())), preferred_element_type=F32)


def lane_block(rows):
    return lax.broadcasted_iota(jnp.int32, (rows, ORB), 1) // 32


def roll(value, blocks):
    blocks = blocks % 4
    return value if blocks == 0 else pltpu.roll(value, 32 * blocks, 1)


def transpose_blocks(parts):
    blk = lane_block(parts[0].shape[0])
    low = blk < 2
    even = (blk % 2) == 0
    a0, a1, a2, a3 = parts
    b0 = jnp.where(low, a0, roll(a2, 2))
    b2 = jnp.where(low, roll(a0, 2), a2)
    b1 = jnp.where(low, a1, roll(a3, 2))
    b3 = jnp.where(low, roll(a1, 2), a3)
    return (
        jnp.where(even, b0, roll(b1, 1)),
        jnp.where(even, roll(b0, 3), b1),
        jnp.where(even, b2, roll(b3, 1)),
        jnp.where(even, roll(b2, 3), b3),
    )


def loop(start, stop, body, unroll=1):
    lax.fori_loop(start, stop, lambda i, c: (body(i), c)[1], 0, unroll=unroll)


def kernel(
    orb, pot, proj, planes_ref, kb, lap, out, gram,
    payload, pot_s16, x_in, r_in, pg, potg, cm, rim, chi_h, chi_l, cht_h, cht_l, pc_mat, wide, base_lv, hl,
    halo_s, halo_r, part, pc_s, pc_r, cc_h, cc_l, fix,
    x_out, r_out, filt, filt_c, xr, xr2, gb, z_r, zs, y_r, ws, x1_r, x2_r, go,
    in_s, in_r, chi_s, chi_r, acr_s, acr_r, cor_s, cor_r, pot_s, pot_r, rim_s, rim_r, hal_s, hal_r, par_s, par_r,
    out_s, out_r, fc_s, fc_r, xs_s, xs_r, rl_s, rl_r, za_s, za_r, zb_s, zb_r, ye_s, ye_r, xe_s, xe_r, zg_s, zg_r, loc, hbm,
):
    middle, scales, recall = filter_terms(DEGREE)
    b = lax.axis_index("band")
    g = lax.axis_index("grid")
    s, y = g // 4, g % 4
    z, xl = s % 8, s // 8
    xh, c = b // 2, b % 2
    core = (2 * xh + 1 - c, g)
    across = (2 * (1 - xh) + c, g)
    cross = (2 * (1 - xh) + 1 - c, g)
    other = (g + 32) % 64
    up = (b, (g + 4) % 64)
    down = (b, (g + 60) % 64)
    ypeer = [None] + [(b, 4 * s + (y + k) % 4) for k in range(1, 4)]
    zpeer = [None] + [(b, 32 * xl + 4 * ((z + k) % 8) + y) for k in range(1, 8)]
    xpeers = [(b, other), across, (across[0], other), cross, (cross[0], other)]
    pending = []

    def rcopy(src, dst, ssem, rsem, dev):
        cp = pltpu.make_async_remote_copy(
            src_ref=src, dst_ref=dst, send_sem=ssem, recv_sem=rsem, device_id=dev, device_id_type=MESH
        )
        cp.start()
        pending.append(cp)
        return cp

    barrier = pltpu.get_barrier_semaphore()
    friends = ypeer[1:] + zpeer[1:] + xpeers + [up, down, core]
    for dev in friends:
        pl.semaphore_signal(barrier, inc=1, device_id=dev, device_id_type=MESH)

    payload[pl.ds(0, 52)] = proj[...]
    payload[pl.ds(54, 2)] = jnp.zeros((2, 8, ROWS), F32)
    for j in range(4):
        payload[52 + j // 2, :, pl.ds(128 * (j % 2), 128)] = jnp.full((8, 128), planes_ref[j, 0].astype(F32))
    p_pick = (
        lax.broadcasted_iota(jnp.int32, (16, ROWS), 1) % 16 == lax.broadcasted_iota(jnp.int32, (16, ROWS), 0)
    )
    p_pick = jnp.where(p_pick, 1.0, 0.0).astype(BF16)
    p_high, p_mid, p_low = split3(pot[...].reshape(16 * CX, 16))
    wide_pot = dot(p_high, p_pick) + (dot(p_mid, p_pick) + dot(p_low, p_pick))
    p_mine = (
        lax.broadcasted_iota(jnp.int32, (16 * CX, ROWS), 1) // 16
        == lax.broadcasted_iota(jnp.int32, (16 * CX, ROWS), 0) % 16
    )
    rows_pot = jnp.sum(jnp.where(p_mine, wide_pot, 0.0).reshape(CX, 16, ROWS), axis=1)
    pot_s16[...] = jnp.concatenate([rows_pot, jnp.zeros((4, ROWS), F32)], axis=0)
    p_row = lax.broadcasted_iota(jnp.int32, (8, ORB), 0)
    kbt = jnp.zeros((8, ORB), F32)
    for p in range(8):
        kbt = jnp.where(p_row == p, kb[p], kbt)
    def pack_in(i):
        parts = [orb[i, pl.ds(QR * q, QR), :] for q in range(4)]
        for k, value in enumerate(transpose_blocks(parts)):
            x_in[k, i] = value

    loop(0, CX, pack_in, 2)
    pl.semaphore_wait(barrier, len(friends))

    mine = pl.ds(14 * b, 14)
    theirs = pl.ds(14 * across[0], 14)
    chi_in = [None]
    pot_in = [None]
    for k in range(1, 4):
        chi_in.append(rcopy(payload.at[mine], pg.at[y, mine], chi_s.at[k - 1], chi_r.at[k - 1], ypeer[k]))
        pot_in.append(rcopy(pot_s16, potg.at[y], pot_s.at[k - 1], pot_r.at[k - 1], ypeer[k]))
    own_pg = pltpu.make_async_copy(payload, pg.at[y], loc.at[0])
    own_pg.start()
    own_pot = pltpu.make_async_copy(pot_s16, potg.at[y], loc.at[1])
    own_pot.start()

    span = CX // CH_IN
    orb_in = []
    orb_own = []

    for ch in range(CH_IN):
        planes = pl.ds(span * ch, span)
        row = []
        for k in range(1, 4):
            row.append(
                rcopy(
                    x_in.at[(y + k) % 4, planes], r_in.at[y, planes],
                    in_s.at[k - 1, ch], in_r.at[k - 1, ch], ypeer[k],
                )
            )
        orb_in.append(row)
        own = pltpu.make_async_copy(x_in.at[y, planes], r_in.at[y, planes], loc.at[2 + ch])
        own.start()
        orb_own.append(own)

    acr_in = []
    cor_in = []
    own_pg.wait()
    for k in range(1, 4):
        chi_in[k].wait_recv()
        src = (y + 4 - k) % 4
        acr_in.append(rcopy(pg.at[src, mine], pg.at[src, mine], acr_s.at[k - 1], acr_r.at[k - 1], across))
        cor_in.append(rcopy(pg.at[src, mine], pg.at[src, mine], cor_s.at[0, k - 1], cor_r.at[0, k - 1], core))
    for slot in range(4, 8):
        potg[slot] = jnp.zeros((16, ROWS), F32)
    own_pot.wait()
    for k in range(1, 4):
        pot_in[k].wait_recv()
    pot_t = potg[...].reshape(128, ROWS).T
    p_high, p_mid, p_low = split3(pot_t)
    centre = 3.0 * HALFW[0] - middle
    e_row = lax.broadcasted_iota(jnp.int32, (128, ORB), 0)
    e_same = (e_row // 16) == lane_block(128)

    def spread_pot(i):
        pick = jnp.where(e_same & (e_row % 16 == i), 1.0, 0.0).astype(BF16)
        pc_mat[i] = (dot(p_high, pick) + (dot(p_mid, pick) + dot(p_low, pick))) + centre

    loop(0, CX, spread_pot)

    for k in range(1, 4):
        acr_in[k - 1].wait_recv()
        src = (y + 4 - k) % 4
        cor_in.append(rcopy(pg.at[src, theirs], pg.at[src, theirs], cor_s.at[1, k - 1], cor_r.at[1, k - 1], core))
    for cp in cor_in:
        cp.wait_recv()

    def place(dom):
        for j in range(4):
            start = pg[dom, 52 + j // 2, :, pl.ds(128 * (j % 2), 128)]
            bits = {}
            left = start
            for size in (8, 4, 2, 1):
                bits[size] = left >= (size - 0.5)
                left = jnp.where(bits[size], left - size, left)
            for lh in range(2):
                lanes = pl.ds(128 * lh, 128)
                zero = jnp.zeros((8, 128), F32)
                rows = [pg[dom, 13 * j + n, :, lanes] for n in range(13)]
                for size in (1, 2, 4, 8):
                    count = min(len(rows) + size, 24)
                    at = lambda n, rows=rows: rows[n] if 0 <= n < len(rows) else zero
                    rows = [jnp.where(bits[size], at(n - size), at(n)) for n in range(count)]
                for n in range(24):
                    cm[dom, n, pl.ds(8 * j, 8), lanes] = rows[n]

    loop(0, 4, place)
    rim_in = [
        rcopy(cm.at[3, pl.ds(18, 6)], rim.at[0], rim_s.at[0], rim_r.at[0], up),
        rcopy(cm.at[0, pl.ds(0, 6)], rim.at[1], rim_s.at[1], rim_r.at[1], down),
    ]

    def make_chi(i, first, blocks):
        mat = jnp.concatenate(blocks, axis=0)
        rows = pl.ds(first, 128)
        chi_h[i, rows, :], chi_l[i, rows, :] = split(mat)
        cht_h[i, :, rows], cht_l[i, :, rows] = split(mat.T)

    loop(0, CX, lambda i: make_chi(i, 0, [cm[d, i + 6] for d in range(4)]))

    for cp in rim_in:
        cp.wait_recv()
    loop(0, 6, lambda i: make_chi(i, 128, [rim[0, i]] + [cm[d, i + 18] for d in range(3)]))
    loop(6, 12, lambda i: make_chi(i, 128, [cm[d, i - 6] for d in range(1, 4)] + [rim[1, i - 6]]))

    def unpack_in(i):
        parts = [r_in[m, i] for m in range(4)]
        for q, value in enumerate(transpose_blocks(parts)):
            wide[0, 6 + i, pl.ds(QR * q, QR), :] = value
            wide[1, 6 + i, pl.ds(QR * q, QR), :] = value

    for ch in range(CH_IN):
        orb_own[ch].wait()
        for cp in orb_in[ch]:
            cp.wait_recv()
        loop(span * ch, span * (ch + 1), unpack_in)

    blk64 = lane_block(QR)
    blk32 = lane_block(NPROJ)

    def send_halo(lv, side, piece):
        planes = (pl.ds(0, 2), pl.ds(2, 4))[piece]
        return rcopy(
            halo_s.at[lv, side, planes], halo_r.at[lv, side, planes],
            hal_s.at[lv, side, piece], hal_r.at[lv, side, piece], (up, down)[side],
        )

    def pack_halo(i):
        high = jnp.zeros((QR, ORB), F32)
        low = jnp.zeros((QR, ORB), F32)
        for q in range(4):
            high = jnp.where(blk64 == q, roll(wide[0, 12 + i, pl.ds(QR * q, QR), :], q - 3), high)
            low = jnp.where(blk64 == q, roll(wide[0, 6 + i, pl.ds(QR * q, QR), :], q), low)
        halo_s[0, 0, i] = high
        halo_s[0, 1, i] = low

    back_in = []
    back_own = []

    def send_out(ch):
        planes = pl.ds(PART_OUT * ch, PART_OUT)
        row = []
        for k in range(1, 4):
            row.append(
                rcopy(
                    x_out.at[(y + k) % 4, planes], r_out.at[y, planes],
                    out_s.at[k - 1, ch], out_r.at[k - 1, ch], ypeer[k],
                )
            )
        back_in.append(row)
        own = pltpu.make_async_copy(x_out.at[y, planes], r_out.at[y, planes], loc.at[8 + ch])
        own.start()
        back_own.append(own)

    loop(0, 6, pack_halo)
    halo_in = [send_halo(0, 0, 0), send_halo(0, 1, 0)]

    def mended(buf, i, edge):
        groups = []
        for q in range(4):
            more = jnp.where(blk64 == edge, roll(fix[i], edge - q), 0.0)
            groups.append(wide[buf, 6 + i, pl.ds(QR * q, QR), :] + more)
        return groups

    for lv in range(DEGREE):
        cur, nxt = lv % 2, 1 - lv % 2
        scale, back = scales[lv], recall[lv]
        part[...] = jnp.zeros_like(part)

        def partials(i):
            for n in range(2):
                at = i + 6 * n
                if lv == 0:
                    value = wide[cur, 6 + at]
                else:
                    value = jnp.concatenate(mended(cur, at, 3 * n), axis=0)
                    wide[cur, 6 + at] = value
                high, low = split(value)
                hl[i, 0, :, pl.ds(ORB * n, ORB)] = high
                hl[i, 1, :, pl.ds(ORB * n, ORB)] = low
                both = dot(chi_h[at], jnp.concatenate([high, low], axis=1))
                value = both[:, :ORB] + (both[:, ORB:] + dot(chi_l[at], high))
                part[0] += value[:128]
                part[1 + n] += value[128:]

        loop(0, 6, partials, 6)
        for n in range(3):
            packed = jnp.zeros((NPROJ, ORB), F32)
            for d in range(4):
                packed = jnp.where(blk32 == d, part[n, pl.ds(NPROJ * d, NPROJ), :], packed)
            pc_s[lv, n] = packed
        own, dn, hi = pc_s[lv, 0], pc_s[lv, 1], pc_s[lv, 2]
        pc_s[lv, 3] = roll(hi, 2) + jnp.where(blk32 == 0, roll(own, 1), 0.0)
        pc_s[lv, 4] = roll(dn, 2) + jnp.where(blk32 == 3, roll(own, 3), 0.0)
        part_in = [
            rcopy(pc_s.at[lv, 3], pc_r.at[lv, 0], par_s.at[lv, 0], par_r.at[lv, 0], up),
            rcopy(pc_s.at[lv, 4], pc_r.at[lv, 1], par_s.at[lv, 1], par_r.at[lv, 1], down),
        ]
        halo_rest = [send_halo(lv, 0, 1), send_halo(lv, 1, 1)]

        def rims(i):
            for q in range(4):
                rows = pl.ds(QR * q, QR)
                wide[cur, i, rows, :] = jnp.where(blk64 == 0, 0.0, roll(wide[cur, 12 + i, rows, :], 1))
                wide[cur, 18 + i, rows, :] = jnp.where(blk64 == 3, 0.0, roll(wide[cur, 6 + i, rows, :], 3))

        loop(0, 6, rims)

        def local(i):
            base_lv[...] = dot3(lap[0], lap[1], hl[i, 0], hl[i, 1])
            for n in range(2):
                at = i + 6 * n
                for q in range(4):
                    rows = pl.ds(QR * q, QR)
                    value = base_lv[rows, pl.ds(ORB * n, ORB)] + pc_mat[at, rows, :] * wide[cur, 6 + at, rows, :]
                    for r in range(1, 7):
                        value = value + HALFW[r] * (wide[cur, 6 + at + r, rows, :] + wide[cur, 6 + at - r, rows, :])
                    value = scale * value
                    if lv > 0:
                        value = value - back * wide[nxt, 6 + at, rows, :]
                    wide[nxt, 6 + at, rows, :] = value

        loop(0, 6, local, 6)
        for cp in part_in:
            cp.wait_recv()
        own, dn, hi = pc_s[lv, 0], pc_s[lv, 1], pc_s[lv, 2]
        below, above = pc_r[lv, 0], pc_r[lv, 1]
        corr = (
            own
            + jnp.where(blk32 == 0, roll(below, 3), roll(hi, 1))
            + jnp.where(blk32 == 3, roll(above, 1), roll(dn, 3))
        )
        corr_low = below + dn
        corr_high = above + hi
        beside_low = jnp.where(blk32 == 0, corr_low, roll(corr, 1))
        beside_high = jnp.where(blk32 == 3, corr_high, roll(corr, 3))
        energy = jnp.concatenate([kbt] * 4, axis=0) * scale
        for n, value in enumerate((corr, beside_low, beside_high)):
            high, low = split(value * energy)
            high, low = high.astype(F32), low.astype(F32)
            for d in range(4):
                rows = pl.ds(NPROJ * d, NPROJ)
                cc_h[n, rows, :] = jnp.where(blk32 == d, high, 0.0).astype(BF16)
                cc_l[n, rows, :] = jnp.where(blk32 == d, low, 0.0).astype(BF16)

        def spread(i, n, edge):
            ch = jnp.concatenate([cc_h[0], cc_h[n]], axis=0)
            cl = jnp.concatenate([cc_l[0], cc_l[n]], axis=0)
            both = dot(cht_h[i], jnp.concatenate([ch, cl], axis=1))
            value = both[:, :ORB] + (both[:, ORB:] + dot(cht_l[i], ch))
            packed = jnp.zeros((QR, ORB), F32)
            for q in range(4):
                rows = pl.ds(QR * q, QR)
                fresh = wide[nxt, 6 + i, rows, :] + value[QR * q : QR * (q + 1)]
                wide[nxt, 6 + i, rows, :] = fresh
                packed = jnp.where(blk64 == q, roll(fresh, q - edge), packed)
            if lv + 1 < DEGREE:
                halo_s[lv + 1, 1 - edge // 3, i - 2 * edge] = packed

        def spread_both(i):
            spread(i, 1, 0)
            spread(6 + i, 2, 3)

        loop(0, 6, spread_both, 6)

        halo_in[0].wait_recv()
        halo_rest[0].wait_recv()
        for i in range(6):
            low = HALFW[i + 1] * halo_r[lv, 0, 5]
            for r in range(i + 2, 7):
                low = low + HALFW[r] * halo_r[lv, 0, 6 + i - r]
            low = scale * low
            fix[i] = low
            if lv + 1 < DEGREE:
                halo_s[lv + 1, 1, i] = halo_s[lv + 1, 1, i] + low
        if lv + 1 < DEGREE:
            downward = send_halo(lv + 1, 1, 0)
        halo_in[1].wait_recv()
        halo_rest[1].wait_recv()
        for i in range(6):
            high = HALFW[6 - i] * halo_r[lv, 1, 0]
            for r in range(7 - i, 7):
                high = high + HALFW[r] * halo_r[lv, 1, i + r - 6]
            high = scale * high
            fix[6 + i] = high
            if lv + 1 < DEGREE:
                halo_s[lv + 1, 0, i] = halo_s[lv + 1, 0, i] + high
        if lv + 1 < DEGREE:
            halo_in = [send_halo(lv + 1, 0, 0), downward]

    for ch in range(CH_OUT):
        for i in range(PART_OUT * ch, PART_OUT * (ch + 1)):
            for k, moved in enumerate(transpose_blocks(mended(DEGREE % 2, i, 3 * (i // 6)))):
                x_out[k, i] = moved
        send_out(ch)

    def unpack_out(i):
        parts = [r_out[m, i] for m in range(4)]
        for q, value in enumerate(transpose_blocks(parts)):
            filt[i, pl.ds(QR * q, QR), :] = value

    gb[...] = jnp.zeros_like(gb)

    def gram_step(slot, lhs, rhs):
        a_high, a_low = split(lhs)
        parts = [split(value) for value in rhs]
        r_high = jnp.concatenate([p[0] for p in parts], axis=1)
        r_low = jnp.concatenate([p[1] for p in parts], axis=1)
        value = dot_t(a_high, r_high) + (dot_t(a_high, r_low) + dot_t(a_low, r_high))
        gb[slot] += value[:, :128]
        gb[slot + 1] += value[:, 128:]

    fc_in = []
    x_recv = []
    stores = []
    relay = []
    keep = pl.ds(128 * xh, 128)
    give = pl.ds(128 * (1 - xh), 128)

    def near(ch):
        fc_in[ch].wait_recv()
        loop(PART_OUT * ch, PART_OUT * (ch + 1), lambda i: gram_step(0, filt[i], [filt[i], filt_c[i]]), PART_OUT)

    def pass_on(ch):
        x_recv[ch].wait_recv()
        planes = pl.ds(PART_OUT * ch, PART_OUT)
        relay.append(rcopy(xr.at[planes], xr2.at[planes], rl_s.at[ch], rl_r.at[ch], core))

    def flat_rows(ref, i, rows):
        return ref[pl.ds(PART_OUT * i, PART_OUT), rows, :].reshape(PART_OUT * 128, ORB)

    for ch in range(CH_OUT):
        back_own[ch].wait()
        for cp in back_in[ch]:
            cp.wait_recv()
        loop(PART_OUT * ch, PART_OUT * (ch + 1), unpack_out, PART_OUT)
        planes = pl.ds(PART_OUT * ch, PART_OUT)
        x_recv.append(rcopy(filt.at[planes, give], xr.at[planes], xs_s.at[ch], xs_r.at[ch], across))
        fc_in.append(rcopy(filt.at[planes], filt_c.at[planes], fc_s.at[ch], fc_r.at[ch], core))
        store = pltpu.make_async_copy(filt.at[planes], out.at[planes], hbm.at[ch])
        store.start()
        stores.append(store)
        if ch > 0:
            near(ch - 1)
        if ch > 2:
            pass_on(ch - 3)
    near(CH_OUT - 1)

    def to_z(first, ssem, rsem):
        for k in range(1, 8):
            pltpu.make_async_remote_copy(
                src_ref=gb.at[pl.ds(first, 2), pl.ds(16 * ((z + k) % 8), 16)], dst_ref=z_r.at[first // 2, k - 1],
                send_sem=ssem, recv_sem=rsem, device_id=zpeer[k], device_id_type=MESH,
            ).start()

    every = pl.ds(0, 128)
    for ch in range(CH_OUT):
        if ch + 3 < CH_OUT:
            pass_on(ch + 3)
        if ch == 0:
            to_z(0, za_s, za_r)
        relay[ch].wait_recv()
        gram_step(2, flat_rows(filt, ch, keep), [flat_rows(xr, ch, every), flat_rows(xr2, ch, every)])
    for n in (2, 3):
        gb[n] = jnp.where(xh == 1, gb[n].T, gb[n])

    to_z(2, zb_s, zb_r)
    tile = pl.ds(16 * z, 16)
    for n, sem in ((0, za_r), (1, zb_r)):
        pltpu.make_async_copy(z_r.at[n], z_r.at[n], sem).wait()
        value = gb[pl.ds(2 * n, 2), tile, :]
        for k in range(7):
            value = value + z_r[n, k]
        zs[pl.ds(2 * n, 2)] = value
    y_in = [rcopy(zs, y_r.at[k - 1], ye_s.at[k - 1], ye_r.at[k - 1], ypeer[k]) for k in range(1, 4)]
    for cp in y_in:
        cp.wait_recv()
    ws[...] = zs[...] + (y_r[0] + (y_r[1] + y_r[2]))
    x_in2 = [rcopy(ws, x1_r, xe_s.at[0], xe_r.at[0], xpeers[0])]
    for k in range(1, 5):
        x_in2.append(rcopy(ws.at[2 + (k - 1) // 2], x2_r.at[k - 1], xe_s.at[k], xe_r.at[k], xpeers[k]))
    for cp in x_in2:
        cp.wait_recv()
    pair = ws[...] + x1_r[...]
    go[pl.ds(0, 2), tile, :] = pair[:2] * (1.0 / CELLS)
    go[2, tile, :] = (pair[2] + (x2_r[0] + x2_r[1])) * (1.0 / CELLS)
    go[3, tile, :] = (pair[3] + (x2_r[2] + x2_r[3])) * (1.0 / CELLS)
    for k in range(1, 8):
        pltpu.make_async_remote_copy(
            src_ref=go.at[:, tile], dst_ref=go.at[:, tile], send_sem=zg_s, recv_sem=zg_r,
            device_id=zpeer[k], device_id_type=MESH,
        ).start()
    pltpu.make_async_copy(z_r, z_r, zg_r).wait()
    for n, dev in enumerate((b, core[0], across[0], cross[0])):
        value = go[n] if n < 2 else jnp.where(xh == 1, go[n].T, go[n])
        gram[:, pl.ds(pl.multiple_of(128 * dev, 128), 128)] = value

    pltpu.make_async_copy(z_r.at[0], z_r.at[0], za_s).wait()
    pltpu.make_async_copy(z_r.at[1], z_r.at[1], zb_s).wait()
    pltpu.make_async_copy(z_r, z_r, zg_s).wait()
    for cp in stores:
        cp.wait()
    for cp in pending:
        cp.wait_send()


def run(orb, pot, proj, planes_ref, kb, lap):
    vmem = functools.partial(pltpu.VMEM)
    dma = pltpu.SemaphoreType.DMA
    f = lambda *shape: vmem(shape, F32)
    h = lambda *shape: vmem(shape, BF16)
    scratch = [
        f(56, 8, ROWS), f(16, ROWS),
        f(4, CX, QR, ORB), f(4, CX, QR, ORB), f(4, 56, 8, ROWS), f(8, 16, ROWS), f(4, 24, NPROJ, ROWS),
        f(2, 6, NPROJ, ROWS), h(CX, ROWS, ROWS), h(CX, ROWS, ROWS), h(CX, ROWS, ROWS), h(CX, ROWS, ROWS),
        f(CX, ROWS, ORB), f(2, 24, ROWS, ORB), f(ROWS, 2 * ORB), h(6, 2, ROWS, 2 * ORB),
        f(DEGREE, 2, 6, QR, ORB), f(DEGREE, 2, 6, QR, ORB), f(3, 128, ORB),
        f(DEGREE, 5, NPROJ, ORB), f(DEGREE, 2, NPROJ, ORB), h(3, 128, ORB), h(3, 128, ORB), f(CX, QR, ORB),
        f(4, CX, QR, ORB), f(4, CX, QR, ORB), f(CX, ROWS, ORB), f(CX, ROWS, ORB), f(CX, 128, ORB), f(CX, 128, ORB),
        f(4, 128, 128), f(2, 7, 2, 16, 128), f(4, 16, 128), f(3, 4, 16, 128), f(4, 16, 128), f(4, 16, 128),
        f(4, 16, 128), f(4, 128, 128),
        dma((3, CH_IN)), dma((3, CH_IN)), dma((3,)), dma((3,)), dma((3,)), dma((3,)), dma((2, 3)), dma((2, 3)),
        dma((3,)), dma((3,)),
        dma((2,)), dma((2,)), dma((DEGREE, 2, 2)), dma((DEGREE, 2, 2)), dma((DEGREE, 2)), dma((DEGREE, 2)),
        dma((3, CH_OUT)), dma((3, CH_OUT)), dma((CH_OUT,)), dma((CH_OUT,)),
        dma((CH_OUT,)), dma((CH_OUT,)), dma((CH_OUT,)), dma((CH_OUT,)),
        dma, dma, dma, dma, dma((3,)), dma((3,)), dma((5,)), dma((5,)), dma, dma, dma((16,)), dma((CH_OUT,)),
    ]
    spec = pl.BlockSpec(memory_space=pltpu.VMEM)
    smem = pl.BlockSpec(memory_space=pltpu.SMEM)
    return pl.pallas_call(
        kernel,
        out_shape=(
            jax.ShapeDtypeStruct((CX, ROWS, ORB), F32),
            jax.ShapeDtypeStruct((128, 512), F32),
        ),
        in_specs=[spec, spec, spec, smem, smem, spec],
        out_specs=(pl.BlockSpec(memory_space=pl.ANY), spec),
        scratch_shapes=scratch,
        compiler_params=pltpu.CompilerParams(
            collective_id=0, has_side_effects=True, vmem_limit_bytes=60 * 2**20
        ),
        name="chebyshev",
    )(orb, pot, proj, planes_ref, kb, lap)


def place_kernel(a, b, a_out, b_out, a_here, b_here, in_sems, out_sems):
    parts = [(a.at[pl.ds(2 * n, 2)], a_here.at[pl.ds(2 * n, 2)], a_out.at[pl.ds(2 * n, 2)]) for n in range(6)]
    parts.append((b, b_here, b_out))
    reads = [pltpu.make_async_copy(src, here, in_sems.at[n]) for n, (src, here, _) in enumerate(parts)]
    writes = [pltpu.make_async_copy(here, dst, out_sems.at[n]) for n, (_, here, dst) in enumerate(parts)]
    for cp in reads:
        cp.start()
    for read, write in zip(reads, writes):
        read.wait()
        write.start()
    for cp in writes:
        cp.wait()


def place_results(a, b):
    spec = pl.BlockSpec(memory_space=pl.ANY)
    return pl.pallas_call(
        place_kernel,
        out_shape=(jax.ShapeDtypeStruct(a.shape, F32), jax.ShapeDtypeStruct(b.shape, F32)),
        in_specs=[spec] * 2,
        out_specs=(spec, spec),
        scratch_shapes=[
            pltpu.VMEM(a.shape, F32), pltpu.VMEM(b.shape, F32),
            pltpu.SemaphoreType.DMA((7,)), pltpu.SemaphoreType.DMA((7,)),
        ],
        compiler_params=pltpu.CompilerParams(vmem_limit_bytes=60 * 2**20),
        name="place",
    )(a, b)


def shards(orbitals, potential, projectors, atom_planes, kb_energy):
    filtered, gram = run(
        orbitals.reshape(CX, ROWS, ORB), potential, projectors.transpose(0, 2, 1, 3).reshape(52, 8, ROWS),
        atom_planes, kb_energy,
        jnp.asarray(plane_laplacian()),
    )
    filtered, gram = place_results(filtered, gram)
    return filtered.reshape(orbitals.shape), gram


def solution(mesh):
    return jax.shard_map(
        shards,
        mesh=mesh,
        in_specs=(
            P("grid", None, None, "band"),
            P("grid", None, None),
            P("grid", None, None, None),
            P("grid", None),
            P(),
        ),
        out_specs=(P("grid", None, None, "band"), P("band", None)),
        check_vma=False,
    )
```
